512 devices in a mesh: rep: 32 (over y_lo, z), ctx: 16 (over y_hi, x, core).
Axes of the slice: x: 4, y: 8 (y_hi: 2, y_lo: 4; y = y_hi * 4 + y_lo), z: 8, core: 2. Of those that a mesh axis runs over, the one named last changes fastest.
Arguments:
- q_first: bfloat16 [64, 4096], P('rep'), as said below
- kv_first: bfloat16 [64, 1024], P('rep'), as said below
- hidden_next: bfloat16 [64, 5120], P('rep', 'ctx'), as said below
- lengths: int32 [64], P('rep'), may hold values from 4096 to 16384, as said below
- owners: int32 [16, 32], P('ctx'), may hold values from 0 to 31, as said below
- sectioned: bfloat16 [32, 160, 5120], P('rep', 'ctx'), as said below
- kv_cache: bfloat16 [64, 2, 16384, 512], P('rep', None, 'ctx'), as said below
Outputs:
- attended: bfloat16 [64, 2, 4096], P('rep')
- kv_second: bfloat16 [64, 1024], P('rep')
The draws below stay inside these ranges and needn't reach their ends.
Inputs may be any that keep to these rules, and one draw needn't show every extreme that they name: `q_first`: queries of the first step. `kv_first`: key and value of the first step's token. `hidden_next`: input rows of the second step. `lengths`: some rollout uses all 16384 positions. Each row of owners is a permutation of the 32 replica slots. `sectioned`: projection rows. `kv_cache`: cached keys and values.
All inputs are finite; a program needn't handle non-finite values.
Results may differ from the reference program's by a relative error of at most 0.007.
Values may be sent and summed in bfloat16 or wider, within the bound.
No kernel may reach another device: no remote copies, remote signals or barrier semaphores. Data moves between devices by JAX's collectives and lax.ppermute only.
A program may use at most 64 MiB of HBM per device.

```python
import jax
import jax.numpy as jnp
from jax import lax

D = 5120
HD = 128
QH = 32
KVH = 4
ROLL_ALL = 64
CTX_ALL = 16384
QKV = 5120
BUCKET_ROWS = 10
N_REP = 32
N_CTX = 16


def shared_queries(key):
    return jax.random.normal(key, (ROLL_ALL, QH * HD), jnp.float32)


def draw_q_first(key, part):
    base = shared_queries(key)
    return base.astype(jnp.bfloat16)


def draw_kv_first(key, part):
    key = jax.random.fold_in(key, 12)
    noise_key, value_key = jax.random.split(key)
    noise = jax.random.normal(noise_key, (ROLL_ALL, KVH * HD), jnp.float32)
    new_values = jax.random.normal(value_key, (ROLL_ALL, KVH * HD), jnp.float32)
    new_keys = noise
    return jnp.concatenate([new_keys, new_values], axis=1).astype(jnp.bfloat16)


def draw_hidden_next(key, part):
    key = jax.random.fold_in(key, 13)
    row_key = jax.random.fold_in(key, 0)
    values = jax.random.normal(row_key, (ROLL_ALL, D), jnp.float32)
    return values.astype(jnp.bfloat16)


def draw_lengths(key, part):
    key = jax.random.fold_in(key, 14)
    base_key, pick_key = jax.random.split(key)
    base = jax.random.randint(base_key, (ROLL_ALL,), CTX_ALL // 4, CTX_ALL + 1)
    chosen = jax.random.randint(pick_key, (), 0, ROLL_ALL)
    return jnp.where(jnp.arange(ROLL_ALL) == chosen, CTX_ALL, base).astype(jnp.int32)


def draw_owners(key, part):
    key = jax.random.fold_in(key, 15)
    row_keys = jax.random.split(key, N_CTX)
    return jax.vmap(lambda row_key: jax.random.permutation(row_key, N_REP))(row_keys).astype(jnp.int32)


def draw_sectioned(key, part):
    key = jax.random.fold_in(key, 16)
    query_key, noise_key, value_key = jax.random.split(key, 3)
    spread = D ** (-0.5)
    rows = D // N_REP
    queries = spread * jax.random.normal(query_key, (N_REP, rows, QH * HD), jnp.float32)
    new_keys = spread * jax.random.normal(noise_key, (N_REP, rows, KVH * HD), jnp.float32)
    new_values = spread * jax.random.normal(value_key, (N_REP, rows, KVH * HD), jnp.float32)
    return jnp.concatenate([queries, new_keys, new_values], axis=2).astype(jnp.bfloat16)


def cache_fields(key, amplitude):
    noise_key, sign_key = jax.random.split(key)
    shape = (ROLL_ALL, 2, CTX_ALL, KVH * HD)
    flips = jax.random.bernoulli(sign_key, 0.5, (ROLL_ALL, 1, 1, KVH * HD))
    signs = jnp.where(flips, 1.0, -1.0).astype(jnp.float32)
    ramp = (jnp.arange(CTX_ALL, dtype=jnp.float32) / (CTX_ALL - 1) - 0.5) * amplitude
    which = (jnp.arange(2) == 1).astype(jnp.float32)
    smooth = which[None, :, None, None] * ramp[None, None, :, None] * signs
    return (noise_key, shape, smooth)


def draw_kv_cache(key, part):
    key = jax.random.fold_in(key, 17)
    noise_key, shape, smooth = cache_fields(key, 3.0)
    rough = jnp.clip(jax.random.normal(noise_key, shape, jnp.float32), -6.0, 6.0)
    return (rough + smooth).astype(jnp.bfloat16)


def setup_inputs(seed: int = 0) -> dict:
    key_list = jax.random.split(jax.random.key(seed), 8)
    q_first = draw_q_first(jax.random.fold_in(key_list[7], 71), 0)
    kv_first = draw_kv_first(jax.random.fold_in(key_list[7], 71), 0)
    hidden_next = draw_hidden_next(jax.random.fold_in(key_list[7], 71), 0)
    lengths = draw_lengths(jax.random.fold_in(key_list[7], 71), 0)
    owners = draw_owners(jax.random.fold_in(key_list[7], 71), 0)
    sectioned = draw_sectioned(jax.random.fold_in(key_list[7], 71), 0)
    kv_cache = draw_kv_cache(jax.random.fold_in(key_list[7], 71), 0)
    return {"q_first": q_first, "kv_first": kv_first, "hidden_next": hidden_next, "lengths": lengths, "owners": owners, "sectioned": sectioned, "kv_cache": kv_cache}


def rotate_pairs(vectors, position):
    halfway = vectors.shape[-1] // 2
    frequency = jnp.power(jnp.float32(1000000.0), -(jnp.arange(halfway, dtype=jnp.float32) * 2.0 / vectors.shape[-1]))
    angles = position * frequency
    cosine = jnp.cos(angles)
    sine_value = jnp.sin(angles)
    first_half = vectors[..., :halfway]
    second_half = vectors[..., halfway:]
    return jnp.concatenate([first_half * cosine - second_half * sine_value, second_half * cosine + first_half * sine_value], axis=-1)


def attend_row(query, cache_keys, cache_values, usable, new_keys, new_values):
    all_keys = jnp.concatenate([cache_keys, new_keys], axis=0).astype(jnp.float32)
    all_values = jnp.concatenate([cache_values, new_values], axis=0).astype(jnp.float32)
    allowed = jnp.concatenate([usable, jnp.ones((new_keys.shape[0],), dtype=bool)])
    grouped = query.reshape(KVH, QH // KVH, HD).astype(jnp.float32)
    scores = jnp.einsum('gqd,kgd->gqk', grouped, all_keys) * (HD ** -0.5)
    scores = jnp.where(allowed, scores, -1e30)
    biggest = jnp.max(scores, axis=-1, keepdims=True)
    exponentials = jnp.exp(scores - biggest)
    totals = jnp.sum(exponentials, axis=-1, keepdims=True)
    rounded = lax.optimization_barrier(exponentials.astype(jnp.bfloat16)).astype(jnp.float32)
    summed = jnp.einsum('gqk,kgd->gqd', rounded, all_values)
    return (summed / totals).reshape(QH * HD)


def reference(q_first, kv_first, hidden_next, lengths, owners, sectioned, kv_cache):
    width_q = QH * HD
    width_kv = KVH * HD
    layered = sectioned.reshape(N_REP, N_CTX, BUCKET_ROWS, QKV)
    weight = layered[owners, jnp.arange(N_CTX, dtype=jnp.int32)[:, None]].reshape(D, QKV)
    projected = jnp.dot(hidden_next, weight, preferred_element_type=jnp.float32)
    position = (lengths + 1).astype(jnp.float32)[:, None, None]
    second_query = rotate_pairs(projected[:, :width_q].reshape(-1, QH, HD), position).astype(jnp.bfloat16)
    second_key = rotate_pairs(projected[:, width_q:width_q + width_kv].reshape(-1, KVH, HD), position).astype(jnp.bfloat16)
    second_value = projected[:, width_q + width_kv:].astype(jnp.bfloat16)
    kv_second = jnp.concatenate([second_key.reshape(-1, width_kv), second_value], axis=1)
    first_key = kv_first[:, :width_kv].reshape(-1, 1, KVH, HD)
    first_value = kv_first[:, width_kv:].reshape(-1, 1, KVH, HD)
    both_keys = jnp.concatenate([first_key, second_key[:, None]], axis=1)
    both_values = jnp.concatenate([first_value, second_value.reshape(-1, 1, KVH, HD)], axis=1)

    def per_rollout(items):
        query_one, query_two, keys_one, values_one, keys_two, values_two, length, cache = items
        cache_keys = cache[0].reshape(CTX_ALL, KVH, HD)
        cache_values = cache[1].reshape(CTX_ALL, KVH, HD)
        usable = jnp.arange(CTX_ALL, dtype=jnp.int32) < length
        out_one = attend_row(query_one.reshape(QH, HD), cache_keys, cache_values, usable, keys_one, values_one)
        out_two = attend_row(query_two, cache_keys, cache_values, usable, keys_two, values_two)
        return jnp.stack([out_one, out_two]).astype(jnp.bfloat16)

    attended = lax.map(per_rollout, (q_first, second_query, first_key, first_value, both_keys, both_values, lengths, kv_cache))
    return attended, kv_second
```

```python
import jax
import jax.numpy as jnp
from jax import lax
from jax.experimental import pallas as pl
from jax.experimental.pallas import tpu as pltpu
from jax.sharding import Mesh, PartitionSpec as P

HD = 128
QH = 32
KVH = 4
GROUP = QH // KVH
HEADS = QH + 2 * KVH
REP = ("yl", "z")
CHIPS = ("yh", "x")
CTX = ("yh", "x", "core")
MASKED = -1e30
VMEM_BYTES = 40 * 1024 * 1024


def spread(rows):
    return jnp.concatenate(
        [jnp.broadcast_to(rows[g : g + 1], (GROUP, HD)) for g in range(KVH)], axis=0
    )


def attend(query, halves, starts, length, extras):
    parts = []
    for (keys, _), start in zip(halves, starts):
        positions = keys.shape[0]
        scores = jnp.concatenate(
            [
                lax.dot_general(
                    query[g * GROUP : (g + 1) * GROUP],
                    keys[:, g * HD : (g + 1) * HD],
                    (((1,), (1,)), ((), ())),
                    preferred_element_type=jnp.float32,
                )
                for g in range(KVH)
            ],
            axis=0,
        ) * HD ** (-0.5)
        position = start + lax.broadcasted_iota(jnp.int32, (1, positions), 1)
        parts.append(jnp.where(position < length, scores, MASKED))
    wide = query.astype(jnp.float32)
    singles = []
    for key_rows, _, counted in extras:
        score = jnp.sum(wide * spread(key_rows.astype(jnp.float32)), axis=1, keepdims=True)
        singles.append(jnp.where(counted, score * HD ** (-0.5), MASKED))
    biggest = jnp.maximum(
        jnp.max(parts[0], axis=1, keepdims=True), jnp.max(parts[1], axis=1, keepdims=True)
    )
    for score in singles:
        biggest = jnp.maximum(biggest, score)
    total = jnp.zeros((QH, 1), jnp.float32)
    summed = jnp.zeros((QH, HD), jnp.float32)
    for part, (_, values) in zip(parts, halves):
        exponentials = jnp.where(part > 0.5 * MASKED, jnp.exp(part - biggest), 0.0)
        total += jnp.sum(exponentials, axis=1, keepdims=True)
        rounded = exponentials.astype(jnp.bfloat16)
        summed += jnp.concatenate(
            [
                jnp.dot(
                    rounded[g * GROUP : (g + 1) * GROUP],
                    values[:, g * HD : (g + 1) * HD],
                    preferred_element_type=jnp.float32,
                )
                for g in range(KVH)
            ],
            axis=0,
        )
    for score, (_, value_rows, _) in zip(singles, extras):
        exponential = jnp.where(score > 0.5 * MASKED, jnp.exp(score - biggest), 0.0)
        total += exponential
        rounded = exponential.astype(jnp.bfloat16).astype(jnp.float32)
        summed += rounded * spread(value_rows.astype(jnp.float32))
    used = total > 0.0
    safe = jnp.where(used, total, 1.0)
    return summed / safe, jnp.where(used, biggest + jnp.log(safe), MASKED)


def as_row(column):
    rows = column.shape[0]
    diagonal = lax.broadcasted_iota(jnp.int32, (rows, HD), 0) == lax.broadcasted_iota(
        jnp.int32, (rows, HD), 1
    )
    return jnp.sum(jnp.where(diagonal, column, 0.0), axis=0, keepdims=True)


def as_column(row, rows):
    diagonal = lax.broadcasted_iota(jnp.int32, (rows, HD), 0) == lax.broadcasted_iota(
        jnp.int32, (rows, HD), 1
    )
    return jnp.sum(jnp.where(diagonal, row, 0.0), axis=1, keepdims=True)


def pack(attended, weight):
    return jnp.concatenate(
        [attended, jnp.broadcast_to(as_row(weight), (8, HD))], axis=0
    )


def halves_of(own, other):
    return ((own.at[0, 0], own.at[0, 1]), (other.at[0], other.at[1]))


def first_kernel(scalars, query, fresh, own, other, out):
    counted = scalars[4] == 0
    attended, weight = attend(
        query[...],
        halves_of(own, other),
        (scalars[1], scalars[2]),
        scalars[3],
        ((fresh[0:KVH], fresh[KVH:], counted),),
    )
    out[...] = pack(attended, weight)


def second_kernel(scalars, shares, cosine, sine, fresh, own, other, out, made):
    counted = scalars[4] == 0
    projected = shares[0]
    for i in range(1, shares.shape[0]):
        projected += shares[i]
    turned = projected[: QH + KVH]
    turned = turned * cosine[...] + pltpu.roll(turned, HD // 2, 1) * sine[...]
    query = turned[:QH].astype(jnp.bfloat16)
    second = jnp.concatenate([turned[QH:], projected[QH + KVH :]], axis=0).astype(jnp.bfloat16)
    made[...] = second
    attended, weight = attend(
        query,
        halves_of(own, other),
        (scalars[1], scalars[2]),
        scalars[3],
        (
            (fresh[0:KVH], fresh[KVH:], counted),
            (second[0:KVH], second[KVH:], counted),
        ),
    )
    out[...] = pack(attended, weight)


def combine_kernel(shares, out):
    count = shares.shape[0]
    for step in range(2):
        weights = [
            as_column(shares[i, step, QH : QH + 1], QH) for i in range(count)
        ]
        biggest = weights[0]
        for weight in weights[1:]:
            biggest = jnp.maximum(biggest, weight)
        total = jnp.zeros((QH, 1), jnp.float32)
        summed = jnp.zeros((QH, HD), jnp.float32)
        for i in range(count):
            scale = jnp.exp(weights[i] - biggest)
            total += scale
            summed += scale * shares[i, step, :QH]
        out[step] = (summed / total).astype(jnp.bfloat16)


def whole(shape):
    return pl.BlockSpec(shape, lambda i, scalars: (0,) * len(shape))


def call_attention(kernel, scalars, smalls, cache, other, out_shape, name):
    own_block = (1,) + cache.shape[1:]
    return pl.pallas_call(
        kernel,
        grid_spec=pltpu.PrefetchScalarGridSpec(
            num_scalar_prefetch=1,
            grid=(1,),
            in_specs=[whole(small.shape) for small in smalls]
            + [
                pl.BlockSpec(own_block, lambda i, scalars: (scalars[0], 0, 0, 0)),
                whole(other.shape),
            ],
            out_specs=[whole(one.shape) for one in out_shape],
        ),
        out_shape=out_shape,
        compiler_params=pltpu.CompilerParams(vmem_limit_bytes=VMEM_BYTES),
        name=name,
    )(scalars, *smalls, cache, other)


def swap(value):
    return lax.ppermute(value, "core", [(0, 1), (1, 0)])


def local(q_first, kv_first, hidden_next, lengths, owners, sectioned, kv_cache):
    rep_size = lax.axis_size(REP)
    chips = lax.axis_size(CHIPS)
    core = lax.axis_index("core")
    chip = lax.axis_index(CHIPS)
    positions = kv_cache.shape[2]
    bucket_rows = sectioned.shape[1]
    width = sectioned.shape[2]

    other_cache = swap(lax.dynamic_index_in_dim(kv_cache, 1 - core, 0, keepdims=False))
    other_rows = swap(sectioned[0])

    selector = (
        owners[0][None, :] == jnp.arange(rep_size, dtype=jnp.int32)[:, None]
    ).astype(jnp.bfloat16)
    by_bucket = hidden_next.reshape(2, rep_size, bucket_rows)
    by_slot = jnp.einsum(
        "sb,rbi->rsi", selector, by_bucket, preferred_element_type=jnp.float32
    ).astype(jnp.bfloat16)
    by_slot = jnp.pad(by_slot, ((0, 0), (0, 0), (0, HD - bucket_rows)))
    hidden = lax.all_to_all(
        by_slot.reshape(2 * rep_size, 1, HD), ("core",) + REP, 0, 0, tiled=True
    ).reshape(2, rep_size, HD)[:, :, :bucket_rows]
    hidden = jnp.where(core == 0, hidden, hidden[::-1])
    partial_sum = jnp.dot(
        jnp.concatenate([hidden[0], hidden[1]], axis=1),
        jnp.concatenate([sectioned[0], other_rows], axis=0),
        preferred_element_type=jnp.float32,
    ).astype(jnp.bfloat16)

    received = lax.all_to_all(
        partial_sum.reshape(rep_size, HEADS, HD), REP, 0, 0, tiled=True
    )
    reduced = jnp.sum(received.astype(jnp.float32), axis=0)
    shares = lax.all_to_all(
        jnp.broadcast_to(reduced[None], (chips, HEADS, HD)), CHIPS, 0, 0, tiled=True
    )

    length = lax.dynamic_index_in_dim(lengths, core, 0, keepdims=False)
    shard = chip * 2 + core
    scalars = jnp.stack(
        [core, shard * positions, (chip * 2 + 1 - core) * positions, length, chip]
    ).astype(jnp.int32)
    frequency = jnp.power(
        jnp.float32(1000000.0), -(jnp.arange(HD // 2, dtype=jnp.float32) * 2.0 / HD)
    )
    angles = (length + 1).astype(jnp.float32) * frequency
    cosine = jnp.cos(angles)
    sine = jnp.sin(angles)
    cosine = jnp.concatenate([cosine, cosine])[None]
    sine = jnp.concatenate([-sine, sine])[None]
    query = lax.dynamic_index_in_dim(q_first, core, 0, keepdims=False).reshape(QH, HD)
    fresh = lax.dynamic_index_in_dim(kv_first, core, 0, keepdims=False).reshape(2 * KVH, HD)

    packed = jax.ShapeDtypeStruct((QH + 8, HD), jnp.float32)
    (first,) = call_attention(
        first_kernel, scalars, (query, fresh), kv_cache, other_cache, (packed,), "first_step"
    )
    second, made = call_attention(
        second_kernel,
        scalars,
        (shares, cosine, sine, fresh),
        kv_cache,
        other_cache,
        (packed, jax.ShapeDtypeStruct((2 * KVH, HD), jnp.bfloat16)),
        "second_step",
    )
    both = jnp.stack([first, second])
    gathered = lax.all_to_all(
        jnp.broadcast_to(both[None], (chips,) + both.shape), CHIPS, 0, 0, tiled=True
    )
    merged = pl.pallas_call(
        combine_kernel,
        out_shape=jax.ShapeDtypeStruct((2, QH, HD), jnp.bfloat16),
        name="combine",
    )(gathered)
    mine = jnp.concatenate([merged.reshape(2 * QH, HD), made], axis=0)
    theirs = swap(mine)
    pair = jnp.where(core == 0, jnp.stack([mine, theirs]), jnp.stack([theirs, mine]))
    attended = pair[:, : 2 * QH].reshape(2, 2, QH * HD)
    kv_second = pair[:, 2 * QH :].reshape(2, 2 * KVH * HD)
    return attended, kv_second


def solution(mesh):
    fine = Mesh(mesh.devices.reshape(4, 8, 2, 4, 2), ("yl", "z", "yh", "x", "core"))
    placed = (
        P(REP, None),
        P(REP, None),
        P(REP, CTX),
        P(REP),
        P(CTX, None),
        P(REP, CTX, None),
        P(REP, None, CTX, None),
    )
    return jax.shard_map(
        local,
        mesh=fine,
        in_specs=placed,
        out_specs=(P(REP, None, None), P(REP, None)),
        check_vma=False,
    )
```

```python
import jax
import jax.numpy as jnp
import numpy as np
from jax import lax
from jax.experimental import pallas as pl
from jax.experimental.pallas import tpu as pltpu
from jax.sharding import Mesh, PartitionSpec as P

HD = 128
QH = 32
KVH = 4
PIECES = 4
GROUP = QH // KVH
HEADS = QH + 2 * KVH
REP = ("yl", "z")
CHIPS = ("yh", "x")
CTX = ("yh", "x", "core")
MASKED = -1e30
VMEM_BYTES = 16 * 1024 * 1024
BETWEEN = 1 << 35
MOST_VMEM = 48 * 1024 * 1024
ALL_VMEM = 60 * 1024 * 1024


def spread(rows):
    return jnp.concatenate(
        [jnp.broadcast_to(rows[g : g + 1], (GROUP, HD)) for g in range(KVH)], axis=0
    )


def fetch(cache, scratch, semaphores):
    core = lax.axis_index("core")
    rows = cache.shape[2] // PIECES
    copies = []
    for kind in range(2):
        for piece in range(PIECES):
            block = pl.ds(piece * rows, rows)
            copies.append(
                pltpu.make_async_copy(
                    cache.at[core, kind, block],
                    scratch.at[kind, block],
                    semaphores.at[kind * PIECES + piece],
                )
            )
    for copy in copies:
        copy.start()
    return copies[:PIECES], copies[PIECES:]


def attend(query, copies, other, scratch, length, extras):
    _, core, chip = place()
    positions = scratch.shape[1]
    halves = (
        (other, (chip * 2 + 1 - core) * positions),
        (scratch, (chip * 2 + core) * positions),
    )
    wide = query.astype(jnp.float32)
    singles = []
    for key_rows, _, counted in extras:
        score = jnp.sum(wide * spread(key_rows.astype(jnp.float32)), axis=1, keepdims=True)
        singles.append(jnp.where(counted, score * HD ** (-0.5), MASKED))
    parts = []
    for cache, start in halves:
        if cache is scratch:
            for copy in copies[0]:
                copy.wait()
        scores = jnp.concatenate(
            [
                lax.dot_general(
                    query[g * GROUP : (g + 1) * GROUP],
                    cache[0, :, g * HD : (g + 1) * HD],
                    (((1,), (1,)), ((), ())),
                    preferred_element_type=jnp.float32,
                )
                for g in range(KVH)
            ],
            axis=0,
        ) * HD ** (-0.5)
        position = start + lax.broadcasted_iota(jnp.int32, (1, positions), 1)
        parts.append(jnp.where(position < length, scores, MASKED))
    biggest = jnp.maximum(
        jnp.max(parts[0], axis=1, keepdims=True), jnp.max(parts[1], axis=1, keepdims=True)
    )
    for score in singles:
        biggest = jnp.maximum(biggest, score)
    total = jnp.zeros((QH, 1), jnp.float32)
    summed = jnp.zeros((QH, HD), jnp.float32)
    for score, (_, value_rows, _) in zip(singles, extras):
        exponential = jnp.where(score > 0.5 * MASKED, jnp.exp(score - biggest), 0.0)
        total += exponential
        rounded = exponential.astype(jnp.bfloat16).astype(jnp.float32)
        summed += rounded * spread(value_rows.astype(jnp.float32))
    for (cache, _), part in zip(halves, parts):
        exponentials = jnp.where(part > 0.5 * MASKED, jnp.exp(part - biggest), 0.0)
        total += jnp.sum(exponentials, axis=1, keepdims=True)
        rounded = exponentials.astype(jnp.bfloat16)
        if cache is scratch:
            for copy in copies[1]:
                copy.wait()
        summed += jnp.concatenate(
            [
                jnp.dot(
                    rounded[g * GROUP : (g + 1) * GROUP],
                    cache[1, :, g * HD : (g + 1) * HD],
                    preferred_element_type=jnp.float32,
                )
                for g in range(KVH)
            ],
            axis=0,
        )
    used = total > 0.0
    safe = jnp.where(used, total, 1.0)
    return summed / safe, jnp.where(used, biggest + jnp.log(safe), MASKED)


def as_row(column):
    rows = column.shape[0]
    diagonal = lax.broadcasted_iota(jnp.int32, (rows, HD), 0) == lax.broadcasted_iota(
        jnp.int32, (rows, HD), 1
    )
    return jnp.sum(jnp.where(diagonal, column, 0.0), axis=0, keepdims=True)


def pad_lanes(row):
    return jnp.concatenate([row, jnp.zeros((1, HD - row.shape[1]), row.dtype)], axis=1)


def as_column(row, rows):
    diagonal = lax.broadcasted_iota(jnp.int32, (rows, HD), 0) == lax.broadcasted_iota(
        jnp.int32, (rows, HD), 1
    )
    return jnp.sum(jnp.where(diagonal, row, 0.0), axis=1, keepdims=True)


def pack(attended, weight):
    return jnp.concatenate([attended, jnp.broadcast_to(as_row(weight), (8, HD))], axis=0)


def place(lengths=None):
    core = lax.axis_index("core")
    return None if lengths is None else lengths[core], core, lax.axis_index(CHIPS)


def stage_kernel(cache, other, scratch, arrived, left):
    core = lax.axis_index("core")
    parts = arrived.shape[0] // 2
    rows = cache.shape[2] // parts
    pieces = [(kind, pl.ds(part * rows, rows)) for kind in range(2) for part in range(parts)]
    inward = [
        pltpu.make_async_copy(cache.at[1 - core, kind, block], scratch.at[kind, block], arrived.at[i])
        for i, (kind, block) in enumerate(pieces)
    ]
    outward = [
        pltpu.make_async_copy(scratch.at[kind, block], other.at[kind, block], left.at[i])
        for i, (kind, block) in enumerate(pieces)
    ]
    for copy in inward:
        copy.start()
    for first, second in zip(inward, outward):
        first.wait()
        second.start()
    for copy in outward:
        copy.wait()


def prepare_kernel(lengths, queries, fresh, frequency, cosine, sine, query, new_rows):
    core = lax.axis_index("core")
    angles = (lengths[core] + 1).astype(jnp.float32) * frequency[...]
    lane = lax.broadcasted_iota(jnp.int32, (1, HD), 1)
    cosine[...] = jnp.cos(angles)
    sine[...] = jnp.where(lane < HD // 2, -1.0, 1.0) * jnp.sin(angles)
    wide = queries[...].astype(jnp.float32)
    wide = jnp.where(core == 0, wide[0:1], wide[1:2])
    query[...] = jnp.concatenate(
        [wide[:, i * HD : (i + 1) * HD] for i in range(QH)], axis=0
    ).astype(jnp.bfloat16)
    wide = fresh[...].astype(jnp.float32)
    wide = jnp.where(core == 0, wide[0:1], wide[1:2])
    new_rows[...] = jnp.concatenate(
        [wide[:, i * HD : (i + 1) * HD] for i in range(2 * KVH)], axis=0
    ).astype(jnp.bfloat16)


def route_kernel(hidden_source, owners_source, out, hidden, owners, semaphores):
    copies = (
        pltpu.make_async_copy(hidden_source, hidden, semaphores.at[0]),
        pltpu.make_async_copy(owners_source, owners, semaphores.at[1]),
    )
    for copy in copies:
        copy.start()
    for copy in copies:
        copy.wait()
    slots = owners.shape[1]
    columns = hidden.shape[1]
    bucket_rows = columns // slots
    column = lax.broadcasted_iota(jnp.int32, (slots, columns), 1)
    first = lax.broadcasted_iota(jnp.int32, (slots, columns), 0) * bucket_rows
    inside = (column >= first) & (column < first + bucket_rows)
    owner = jnp.sum(
        jnp.where(inside, as_column(pad_lanes(owners[...].astype(jnp.float32)), slots), 0.0),
        axis=0,
        keepdims=True,
    )
    chosen = owner == lax.broadcasted_iota(jnp.int32, (slots, columns), 0).astype(jnp.float32)
    row = lax.broadcasted_iota(jnp.int32, (columns, HD), 0)
    lane = lax.broadcasted_iota(jnp.int32, (columns, HD), 1)
    bucket = jnp.floor((row.astype(jnp.float32) + 0.5) * (1.0 / bucket_rows)).astype(jnp.int32)
    fold = row == lane + bucket * bucket_rows
    fold = jnp.where(fold, 1.0, 0.0).astype(jnp.bfloat16)
    for core in range(2):
        kept = jnp.where(chosen, hidden[core : core + 1].astype(jnp.float32), 0.0)
        folded = jnp.dot(kept.astype(jnp.bfloat16), fold, preferred_element_type=jnp.float32)
        out[core * slots : (core + 1) * slots] = jnp.broadcast_to(
            folded[:, None, :], (slots, 2, HD)
        )


def project_kernel(hidden, own_rows, other_rows, out, rows, wide):
    core = lax.axis_index("core")
    bucket_rows = own_rows.shape[0]
    slots = out.shape[0]
    rows[...] = jnp.zeros_like(rows)
    rows[0:bucket_rows] = own_rows[...]
    rows[16 : 16 + bucket_rows] = other_rows[...]
    received = hidden[:, 0, :].astype(jnp.bfloat16)
    own = jnp.where(core == 0, received[:slots], received[slots:])[:, :16]
    other = jnp.where(core == 0, received[slots:], received[:slots])[:, :16]
    both = jnp.concatenate([own, other], axis=1)
    step = 8
    for start in range(0, out.shape[1], step):
        block = jnp.dot(
            both,
            rows[:, start * HD : (start + step) * HD],
            preferred_element_type=jnp.float32,
        )
        for i in range(step):
            wide[:, start + i, :] = block[:, i * HD : (i + 1) * HD]
    out[...] = wide[...].astype(jnp.bfloat16)


def reduce_kernel(received, out):
    total = received[0].astype(jnp.float32)
    for i in range(1, received.shape[0]):
        total += received[i].astype(jnp.float32)
    for i in range(out.shape[0]):
        out[i] = total


def first_kernel(lengths, query, fresh, cache, other, out, scratch, semaphores):
    copies = fetch(cache, scratch, semaphores)
    length, _, chip = place(lengths)
    attended, weight = attend(
        query[...],
        copies,
        other,
        scratch,
        length,
        ((fresh[0:KVH], fresh[KVH:], chip == 0),),
    )
    out[...] = pack(attended, weight)


def second_kernel(
    lengths, shares, cosine, sine, fresh, first, cache, other, out, scratch, semaphores
):
    copies = fetch(cache, scratch, semaphores)
    length, _, chip = place(lengths)
    projected = shares[0]
    for i in range(1, shares.shape[0]):
        projected += shares[i]
    turned = projected[: QH + KVH]
    turned = turned * cosine[...] + pltpu.roll(turned, HD // 2, 1) * sine[...]
    query = turned[:QH].astype(jnp.bfloat16)
    second = jnp.concatenate([turned[QH:], projected[QH + KVH :]], axis=0)
    rounded = second.astype(jnp.bfloat16)
    attended, weight = attend(
        query,
        copies,
        other,
        scratch,
        length,
        (
            (fresh[0:KVH], fresh[KVH:], chip == 0),
            (rounded[0:KVH], rounded[KVH:], chip == 0),
        ),
    )
    weights = as_row(jnp.concatenate([as_column(first[QH : QH + 1], QH), weight], axis=0))
    high = weights.astype(jnp.bfloat16).astype(jnp.float32)
    middle = (weights - high).astype(jnp.bfloat16).astype(jnp.float32)
    low = weights - high - middle
    payload = jnp.concatenate(
        [first[:QH], attended, second, high, middle, low, jnp.zeros((5, HD), jnp.float32)], axis=0
    ).astype(jnp.bfloat16)
    for i in range(out.shape[0]):
        out[i] = payload


def flat(rows):
    return jnp.concatenate([rows[i : i + 1] for i in range(rows.shape[0])], axis=1)


def combine_kernel(shares, attended, made):
    count = shares.shape[0] // 2
    heads = 2 * QH
    fresh = []
    for core in range(2):
        weights = []
        for i in range(count):
            share = shares[2 * i + core]
            pieces = share[heads + 2 * KVH :].astype(jnp.float32)
            weights.append(as_column(pieces[0:1] + pieces[1:2] + pieces[2:3], heads))
        biggest = weights[0]
        for weight in weights[1:]:
            biggest = jnp.maximum(biggest, weight)
        total = jnp.zeros((heads, 1), jnp.float32)
        summed = jnp.zeros((heads, HD), jnp.float32)
        for i in range(count):
            scale = jnp.exp(weights[i] - biggest)
            total += scale
            summed += scale * shares[2 * i + core, :heads].astype(jnp.float32)
        merged = summed / total
        attended[core] = jnp.concatenate([flat(merged[:QH]), flat(merged[QH:])], axis=0).astype(
            jnp.bfloat16
        )
        fresh.append(flat(shares[core, heads : heads + 2 * KVH].astype(jnp.float32)))
    made[...] = jnp.concatenate(fresh, axis=0).astype(jnp.bfloat16)


def kernel_call(
    kernel, out_shape, name, operands, spaces="", scratch=(), limit=VMEM_BYTES, work=0
):
    kinds = {"v": pltpu.VMEM, "s": pltpu.SMEM, "h": pltpu.HBM}
    spaces = spaces or "v" * len(operands)
    moved = sum(one.size * one.dtype.itemsize for one in (*operands, *out_shape))
    return pl.pallas_call(
        kernel,
        in_specs=[pl.BlockSpec(memory_space=kinds[one]) for one in spaces],
        out_specs=[pl.BlockSpec(memory_space=pltpu.VMEM)] * len(out_shape),
        out_shape=out_shape,
        scratch_shapes=scratch,
        compiler_params=pltpu.CompilerParams(vmem_limit_bytes=limit),
        cost_estimate=pl.CostEstimate(flops=work, bytes_accessed=moved, transcendentals=0),
        name=name,
    )(*operands)


def swap(value):
    return lax.ppermute(value, "core", [(0, 1), (1, 0)])


def local(q_first, kv_first, hidden_next, lengths, owners, sectioned, kv_cache):
    rep_size = lax.axis_size(REP)
    chips = lax.axis_size(CHIPS)
    core = lax.axis_index("core")
    bf16, f32 = jnp.bfloat16, jnp.float32
    shape = jax.ShapeDtypeStruct
    _, _, positions, columns = kv_cache.shape

    (by_slot,) = kernel_call(
        route_kernel,
        (shape((2 * rep_size, 2, HD), f32),),
        "route_hidden",
        (hidden_next, owners),
        spaces="hh",
        scratch=[
            pltpu.VMEM(hidden_next.shape, bf16),
            pltpu.VMEM(owners.shape, jnp.int32),
            pltpu.SemaphoreType.DMA((2,)),
        ],
        limit=ALL_VMEM,
    )
    by_slot, sectioned, kv_cache = lax.optimization_barrier((by_slot, sectioned, kv_cache))
    hidden = lax.all_to_all(by_slot, ("core",) + REP, 0, 0, tiled=True)
    other_rows = swap(sectioned[0])
    staged = pl.pallas_call(
        stage_kernel,
        in_specs=[pl.BlockSpec(memory_space=pltpu.HBM)],
        out_specs=pl.BlockSpec(memory_space=pltpu.HBM),
        out_shape=shape(kv_cache.shape[1:], bf16),
        scratch_shapes=[
            pltpu.VMEM(kv_cache.shape[1:], bf16),
            pltpu.SemaphoreType.DMA((4,)),
            pltpu.SemaphoreType.DMA((4,)),
        ],
        compiler_params=pltpu.CompilerParams(vmem_limit_bytes=ALL_VMEM),
        cost_estimate=pl.CostEstimate(flops=0, bytes_accessed=8 * positions * columns, transcendentals=0),
        name="stage_cache",
    )(kv_cache)
    hidden, other_rows, staged = lax.optimization_barrier((hidden, other_rows, staged))
    (partial_sum,) = kernel_call(
        project_kernel,
        (shape((rep_size, HEADS, HD), bf16),),
        "project",
        (hidden, sectioned[0], other_rows),
        scratch=[
            pltpu.VMEM((32, HEADS * HD), bf16),
            pltpu.VMEM((rep_size, HEADS, HD), f32),
        ],
    )
    received = lax.all_to_all(partial_sum, REP, 0, 0, tiled=True)
    other_cache = swap(staged)

    halved = np.float32(1000000.0) ** (-(np.arange(HD // 2, dtype=np.float32) * 2.0 / HD))
    frequency = jnp.asarray(np.concatenate([halved, halved])[None], f32)
    cosine, sine, query, fresh = kernel_call(
        prepare_kernel,
        (shape((1, HD), f32), shape((1, HD), f32), shape((QH, HD), bf16), shape((2 * KVH, HD), bf16)),
        "prepare_rows",
        (lengths, q_first, kv_first, frequency),
        spaces="svvv",
        work=BETWEEN,
    )
    attention_scratch = [
        pltpu.VMEM((2, positions, columns), bf16),
        pltpu.SemaphoreType.DMA((2 * PIECES,)),
    ]
    (first,) = kernel_call(
        first_kernel,
        (shape((QH + 8, HD), f32),),
        "first_step",
        (lengths, query, fresh, kv_cache, other_cache),
        spaces="svvhv",
        scratch=attention_scratch,
        limit=MOST_VMEM,
    )
    received, first, cosine, sine = lax.optimization_barrier((received, first, cosine, sine))
    (reduced,) = kernel_call(
        reduce_kernel, (shape((chips, HEADS, HD), f32),), "sum_over_replicas", (received,)
    )
    shares = lax.all_to_all(reduced, CHIPS, 0, 0, tiled=True)
    (payload,) = kernel_call(
        second_kernel,
        (shape((2 * chips, 80, HD), bf16),),
        "second_step",
        (lengths, shares, cosine, sine, fresh, first, kv_cache, other_cache),
        spaces="svvvvvhv",
        scratch=attention_scratch,
        limit=MOST_VMEM,
    )
    gathered = lax.all_to_all(payload, CTX, 0, 0, tiled=True)
    attended, made = kernel_call(
        combine_kernel,
        (shape((2, 2, QH * HD), bf16), shape((2, 2 * KVH * HD), bf16)),
        "combine",
        (gathered,),
    )
    return attended, made


def solution(mesh):
    fine = Mesh(mesh.devices.reshape(4, 8, 2, 4, 2), ("yl", "z", "yh", "x", "core"))
    placed = (
        P(REP, None),
        P(REP, None),
        P(REP, CTX),
        P(REP),
        P(CTX, None),
        P(REP, CTX, None),
        P(REP, None, CTX, None),
    )
    return jax.shard_map(
        local,
        mesh=fine,
        in_specs=placed,
        out_specs=(P(REP, None, None), P(REP, None)),
        check_vma=False,
    )
```

```python
import jax
import jax.numpy as jnp
import numpy as np
from jax import lax
from jax.experimental import pallas as pl
from jax.experimental.pallas import tpu as pltpu
from jax.sharding import Mesh, PartitionSpec as P

HD = 128
QH = 32
KVH = 4
GROUP = QH // KVH
HEADS = QH + 2 * KVH
REP = ("yl", "z")
CHIPS = ("yh", "x")
CTX = ("yh", "x", "core")
MASKED = -1e30
VMEM_BYTES = 16 * 1024 * 1024
BETWEEN = 1 << 36
MOST_VMEM = 48 * 1024 * 1024
ALL_VMEM = 60 * 1024 * 1024


def spread(rows):
    return jnp.concatenate(
        [jnp.broadcast_to(rows[g : g + 1], (2 * GROUP, HD)) for g in range(KVH)], axis=0
    )


def joint(first, second):
    pieces = []
    for g in range(KVH):
        pieces += [first[g * GROUP : (g + 1) * GROUP], second[g * GROUP : (g + 1) * GROUP]]
    return jnp.concatenate(pieces, axis=0)


def by_step(rows):
    return jnp.concatenate(
        [
            rows[(2 * g + step) * GROUP : (2 * g + step + 1) * GROUP]
            for step in range(2)
            for g in range(KVH)
        ],
        axis=0,
    )


def scored(query, keys, start, length):
    scores = jnp.concatenate(
        [
            lax.dot_general(
                query[2 * g * GROUP : 2 * (g + 1) * GROUP],
                keys[:, g * HD : (g + 1) * HD],
                (((1,), (1,)), ((), ())),
                preferred_element_type=jnp.float32,
            )
            for g in range(KVH)
        ],
        axis=0,
    ) * HD ** (-0.5)
    position = start + lax.broadcasted_iota(jnp.int32, (1, keys.shape[0]), 1)
    return jnp.where(position < length, scores, MASKED)


def weighted(rounded, values):
    return jnp.concatenate(
        [
            jnp.dot(
                rounded[2 * g * GROUP : 2 * (g + 1) * GROUP],
                values[:, g * HD : (g + 1) * HD],
                preferred_element_type=jnp.float32,
            )
            for g in range(KVH)
        ],
        axis=0,
    )


def as_row(column):
    rows = column.shape[0]
    diagonal = lax.broadcasted_iota(jnp.int32, (rows, HD), 0) == lax.broadcasted_iota(
        jnp.int32, (rows, HD), 1
    )
    return jnp.sum(jnp.where(diagonal, column, 0.0), axis=0, keepdims=True)


def pad_lanes(row):
    return jnp.concatenate([row, jnp.zeros((1, HD - row.shape[1]), row.dtype)], axis=1)


def as_column(row, rows):
    diagonal = lax.broadcasted_iota(jnp.int32, (rows, HD), 0) == lax.broadcasted_iota(
        jnp.int32, (rows, HD), 1
    )
    return jnp.sum(jnp.where(diagonal, row, 0.0), axis=1, keepdims=True)


def stage_kernel(cache, other, scratch, arrived, left):
    core = lax.axis_index("core")
    parts = arrived.shape[0] // 2
    rows = cache.shape[2] // parts
    pieces = [(kind, pl.ds(part * rows, rows)) for kind in range(2) for part in range(parts)]
    inward = [
        pltpu.make_async_copy(cache.at[1 - core, kind, block], scratch.at[kind, block], arrived.at[i])
        for i, (kind, block) in enumerate(pieces)
    ]
    outward = [
        pltpu.make_async_copy(scratch.at[kind, block], other.at[kind, block], left.at[i])
        for i, (kind, block) in enumerate(pieces)
    ]
    for copy in inward:
        copy.start()
    for first, second in zip(inward, outward):
        first.wait()
        second.start()
    for copy in outward:
        copy.wait()


def prepare_kernel(
    lengths, queries, fresh, frequency, cache, length, cosine, sine, query, new_rows, own_keys, semaphore
):
    core = lax.axis_index("core")
    copy = pltpu.make_async_copy(cache.at[core, 0], own_keys, semaphore)
    copy.start()
    length[...] = jnp.zeros_like(length) + lengths[core]
    angles = (lengths[core] + 1).astype(jnp.float32) * frequency[...]
    lane = lax.broadcasted_iota(jnp.int32, (1, HD), 1)
    cosine[...] = jnp.cos(angles)
    sine[...] = jnp.where(lane < HD // 2, -1.0, 1.0) * jnp.sin(angles)
    wide = queries[...].astype(jnp.float32)
    wide = jnp.where(core == 0, wide[0:1], wide[1:2])
    query[...] = jnp.concatenate(
        [wide[:, i * HD : (i + 1) * HD] for i in range(QH)], axis=0
    ).astype(jnp.bfloat16)
    wide = fresh[...].astype(jnp.float32)
    wide = jnp.where(core == 0, wide[0:1], wide[1:2])
    new_rows[...] = jnp.concatenate(
        [wide[:, i * HD : (i + 1) * HD] for i in range(2 * KVH)], axis=0
    ).astype(jnp.bfloat16)
    copy.wait()


def route_kernel(hidden_source, owners_source, out, hidden, owners, semaphores):
    copies = (
        pltpu.make_async_copy(hidden_source, hidden, semaphores.at[0]),
        pltpu.make_async_copy(owners_source, owners, semaphores.at[1]),
    )
    for copy in copies:
        copy.start()
    for copy in copies:
        copy.wait()
    slots = owners.shape[1]
    columns = hidden.shape[1]
    bucket_rows = columns // slots
    column = lax.broadcasted_iota(jnp.int32, (slots, columns), 1)
    first = lax.broadcasted_iota(jnp.int32, (slots, columns), 0) * bucket_rows
    inside = (column >= first) & (column < first + bucket_rows)
    owner = jnp.sum(
        jnp.where(inside, as_column(pad_lanes(owners[...].astype(jnp.float32)), slots), 0.0),
        axis=0,
        keepdims=True,
    )
    chosen = owner == lax.broadcasted_iota(jnp.int32, (slots, columns), 0).astype(jnp.float32)
    row = lax.broadcasted_iota(jnp.int32, (columns, HD), 0)
    lane = lax.broadcasted_iota(jnp.int32, (columns, HD), 1)
    bucket = jnp.floor((row.astype(jnp.float32) + 0.5) * (1.0 / bucket_rows)).astype(jnp.int32)
    fold = row == lane + bucket * bucket_rows
    fold = jnp.where(fold, 1.0, 0.0).astype(jnp.bfloat16)
    for core in range(2):
        kept = jnp.where(chosen, hidden[core : core + 1].astype(jnp.float32), 0.0)
        folded = jnp.dot(kept.astype(jnp.bfloat16), fold, preferred_element_type=jnp.float32)
        out[core * slots : (core + 1) * slots] = jnp.broadcast_to(
            folded[:, None, :], (slots, 2, HD)
        )


def project_kernel(hidden, own_rows, other_rows, out, rows, wide):
    core = lax.axis_index("core")
    bucket_rows = own_rows.shape[0]
    slots = out.shape[0]
    rows[...] = jnp.zeros_like(rows)
    rows[0:bucket_rows] = own_rows[...]
    rows[16 : 16 + bucket_rows] = other_rows[...]
    received = hidden[:, 0, :].astype(jnp.bfloat16)
    own = jnp.where(core == 0, received[:slots], received[slots:])[:, :16]
    other = jnp.where(core == 0, received[slots:], received[:slots])[:, :16]
    both = jnp.concatenate([own, other], axis=1)
    step = 8
    for start in range(0, out.shape[1], step):
        block = jnp.dot(
            both,
            rows[:, start * HD : (start + step) * HD],
            preferred_element_type=jnp.float32,
        )
        for i in range(step):
            wide[:, start + i, :] = block[:, i * HD : (i + 1) * HD]
    out[...] = wide[...].astype(jnp.bfloat16)


def reduce_kernel(received, out):
    total = received[0].astype(jnp.float32)
    for i in range(1, received.shape[0]):
        total += received[i].astype(jnp.float32)
    for i in range(out.shape[0]):
        out[i] = total


def steps_kernel(
    length, shares, cosine, sine, first_query, fresh, cache, other, own_keys, out, own_values,
    held, kept, semaphore,
):
    core = lax.axis_index("core")
    chip = lax.axis_index(CHIPS)
    positions = own_keys.shape[0]
    copy = pltpu.make_async_copy(cache.at[core, 1], own_values, semaphore)
    copy.start()

    projected = shares[0]
    for i in range(1, shares.shape[0]):
        projected += shares[i]
    turned = projected[: QH + KVH]
    turned = turned * cosine[...] + pltpu.roll(turned, HD // 2, 1) * sine[...]
    second = jnp.concatenate([turned[QH:], projected[QH + KVH :]], axis=0)
    query = joint(first_query[...].astype(jnp.float32), turned[:QH]).astype(jnp.bfloat16)
    limit = length[:, 0:1]
    parts = [
        scored(query, other.at[0], (chip * 2 + 1 - core) * positions, limit),
        scored(query, own_keys, (chip * 2 + core) * positions, limit),
    ]

    wide = query.astype(jnp.float32)
    rows = 2 * QH
    step = (lax.broadcasted_iota(jnp.int32, (rows, 1), 0) // GROUP) % 2
    earlier = fresh[...].astype(jnp.float32)
    later = second.astype(jnp.bfloat16).astype(jnp.float32)
    extras = []
    for token, counted in ((earlier, step >= 0), (later, step == 1)):
        score = jnp.sum(wide * spread(token[:KVH]), axis=1, keepdims=True) * HD ** (-0.5)
        extras.append(jnp.where(counted & (chip == 0), score, MASKED))

    biggest = jnp.maximum(extras[0], extras[1])
    for part in parts:
        biggest = jnp.maximum(biggest, jnp.max(part, axis=1, keepdims=True))
    total = jnp.zeros((rows, 1), jnp.float32)
    summed = jnp.zeros((rows, HD), jnp.float32)
    for score, token in zip(extras, (earlier, later)):
        exponential = jnp.where(score > 0.5 * MASKED, jnp.exp(score - biggest), 0.0)
        total += exponential
        summed += exponential.astype(jnp.bfloat16).astype(jnp.float32) * spread(token[KVH:])
    rounded = []
    for part in parts:
        exponentials = jnp.where(part > 0.5 * MASKED, jnp.exp(part - biggest), 0.0)
        total += jnp.sum(exponentials, axis=1, keepdims=True)
        rounded.append(exponentials.astype(jnp.bfloat16))
    summed += weighted(rounded[0], other.at[1])
    used = total > 0.0
    safe = jnp.where(used, total, 1.0)
    held[0] = summed
    held[1] = jnp.broadcast_to(1.0 / safe, (rows, HD))
    weights = as_row(by_step(jnp.where(used, biggest + jnp.log(safe), MASKED)))
    high = weights.astype(jnp.bfloat16).astype(jnp.float32)
    middle = (weights - high).astype(jnp.bfloat16).astype(jnp.float32)
    low = weights - high - middle
    tail = jnp.concatenate([second, high, middle, low, jnp.zeros((5, HD), jnp.float32)], axis=0)
    tail = tail.astype(jnp.bfloat16)
    for i in range(out.shape[0]):
        out[i, rows:] = tail
    kept[...] = rounded[1]

    @pl.when(chip >= 0)
    def _():
        copy.wait()
        attended = (held[0] + weighted(kept[...], own_values)) * held[1]
        attended = by_step(attended).astype(jnp.bfloat16)
        for i in range(out.shape[0]):
            out[i, :rows] = attended


def flat(rows):
    return jnp.concatenate([rows[i : i + 1] for i in range(rows.shape[0])], axis=1)


def combine_kernel(shares, attended, made):
    count = shares.shape[0] // 2
    heads = 2 * QH
    fresh = []
    for core in range(2):
        weights = []
        for i in range(count):
            share = shares[2 * i + core]
            pieces = share[heads + 2 * KVH :].astype(jnp.float32)
            weights.append(as_column(pieces[0:1] + pieces[1:2] + pieces[2:3], heads))
        biggest = weights[0]
        for weight in weights[1:]:
            biggest = jnp.maximum(biggest, weight)
        total = jnp.zeros((heads, 1), jnp.float32)
        summed = jnp.zeros((heads, HD), jnp.float32)
        for i in range(count):
            scale = jnp.exp(weights[i] - biggest)
            total += scale
            summed += scale * shares[2 * i + core, :heads].astype(jnp.float32)
        merged = summed / total
        attended[core] = jnp.concatenate([flat(merged[:QH]), flat(merged[QH:])], axis=0).astype(
            jnp.bfloat16
        )
        fresh.append(flat(shares[core, heads : heads + 2 * KVH].astype(jnp.float32)))
    made[...] = jnp.concatenate(fresh, axis=0).astype(jnp.bfloat16)


def kernel_call(
    kernel, out_shape, name, operands, spaces="", scratch=(), limit=VMEM_BYTES, work=0
):
    kinds = {"v": pltpu.VMEM, "s": pltpu.SMEM, "h": pltpu.HBM}
    spaces = spaces or "v" * len(operands)
    moved = sum(one.size * one.dtype.itemsize for one in (*operands, *out_shape))
    return pl.pallas_call(
        kernel,
        in_specs=[pl.BlockSpec(memory_space=kinds[one]) for one in spaces],
        out_specs=[pl.BlockSpec(memory_space=pltpu.VMEM)] * len(out_shape),
        out_shape=out_shape,
        scratch_shapes=scratch,
        compiler_params=pltpu.CompilerParams(vmem_limit_bytes=limit),
        cost_estimate=pl.CostEstimate(flops=work, bytes_accessed=moved, transcendentals=0),
        name=name,
    )(*operands)


def swap(value):
    return lax.ppermute(value, "core", [(0, 1), (1, 0)])


def local(q_first, kv_first, hidden_next, lengths, owners, sectioned, kv_cache):
    rep_size = lax.axis_size(REP)
    chips = lax.axis_size(CHIPS)
    core = lax.axis_index("core")
    bf16, f32 = jnp.bfloat16, jnp.float32
    shape = jax.ShapeDtypeStruct
    _, _, positions, columns = kv_cache.shape

    (by_slot,) = kernel_call(
        route_kernel,
        (shape((2 * rep_size, 2, HD), f32),),
        "route_hidden",
        (hidden_next, owners),
        spaces="hh",
        scratch=[
            pltpu.VMEM(hidden_next.shape, bf16),
            pltpu.VMEM(owners.shape, jnp.int32),
            pltpu.SemaphoreType.DMA((2,)),
        ],
        limit=ALL_VMEM,
    )
    by_slot, sectioned, kv_cache = lax.optimization_barrier((by_slot, sectioned, kv_cache))
    hidden = lax.all_to_all(by_slot, ("core",) + REP, 0, 0, tiled=True)
    other_rows = swap(sectioned[0])
    staged = pl.pallas_call(
        stage_kernel,
        in_specs=[pl.BlockSpec(memory_space=pltpu.HBM)],
        out_specs=pl.BlockSpec(memory_space=pltpu.HBM),
        out_shape=shape(kv_cache.shape[1:], bf16),
        scratch_shapes=[
            pltpu.VMEM(kv_cache.shape[1:], bf16),
            pltpu.SemaphoreType.DMA((4,)),
            pltpu.SemaphoreType.DMA((4,)),
        ],
        compiler_params=pltpu.CompilerParams(vmem_limit_bytes=ALL_VMEM),
        cost_estimate=pl.CostEstimate(flops=0, bytes_accessed=8 * positions * columns, transcendentals=0),
        name="stage_cache",
    )(kv_cache)
    hidden, other_rows, _ = lax.optimization_barrier((hidden, other_rows, staged))
    (partial_sum,) = kernel_call(
        project_kernel,
        (shape((rep_size, HEADS, HD), bf16),),
        "project",
        (hidden, sectioned[0], other_rows),
        scratch=[
            pltpu.VMEM((32, HEADS * HD), bf16),
            pltpu.VMEM((rep_size, HEADS, HD), f32),
        ],
    )
    partial_sum, staged = lax.optimization_barrier((partial_sum, staged))
    received = lax.all_to_all(partial_sum, REP, 0, 0, tiled=True)
    other_cache = swap(staged)

    halved = np.float32(1000000.0) ** (-(np.arange(HD // 2, dtype=np.float32) * 2.0 / HD))
    frequency = jnp.asarray(np.concatenate([halved, halved])[None], f32)
    length, cosine, sine, query, fresh, own_keys = kernel_call(
        prepare_kernel,
        (
            shape((1, HD), jnp.int32),
            shape((1, HD), f32),
            shape((1, HD), f32),
            shape((QH, HD), bf16),
            shape((2 * KVH, HD), bf16),
            shape((positions, columns), bf16),
        ),
        "prepare_rows",
        (lengths, q_first, kv_first, frequency, kv_cache),
        spaces="svvvh",
        scratch=[pltpu.SemaphoreType.DMA],
        limit=52 * 1024 * 1024,
        work=BETWEEN,
    )
    received, length = lax.optimization_barrier((received, length))
    (reduced,) = kernel_call(
        reduce_kernel, (shape((chips, HEADS, HD), f32),), "sum_over_replicas", (received,)
    )
    shares = lax.all_to_all(reduced, CHIPS, 0, 0, tiled=True)
    (payload,) = kernel_call(
        steps_kernel,
        (shape((2 * chips, 80, HD), bf16),),
        "both_steps",
        (length, shares, cosine, sine, query, fresh, kv_cache, other_cache, own_keys),
        spaces="vvvvvvhvv",
        scratch=[
            pltpu.VMEM((positions, columns), bf16),
            pltpu.VMEM((2, 2 * QH, HD), f32),
            pltpu.VMEM((2 * QH, positions), bf16),
            pltpu.SemaphoreType.DMA,
        ],
        limit=MOST_VMEM,
    )
    gathered = lax.all_to_all(payload, CTX, 0, 0, tiled=True)
    attended, made = kernel_call(
        combine_kernel,
        (shape((2, 2, QH * HD), bf16), shape((2, 2 * KVH * HD), bf16)),
        "combine",
        (gathered,),
    )
    return attended, made


def solution(mesh):
    fine = Mesh(mesh.devices.reshape(4, 8, 2, 4, 2), ("yl", "z", "yh", "x", "core"))
    placed = (
        P(REP, None),
        P(REP, None),
        P(REP, CTX),
        P(REP),
        P(CTX, None),
        P(REP, CTX, None),
        P(REP, None, CTX, None),
    )
    return jax.shard_map(
        local,
        mesh=fine,
        in_specs=placed,
        out_specs=(P(REP, None, None), P(REP, None)),
        check_vma=False,
    )
```

```python
import jax
import jax.numpy as jnp
import numpy as np
from jax import lax
from jax.experimental import pallas as pl
from jax.experimental.pallas import tpu as pltpu
from jax.sharding import Mesh, PartitionSpec as P

HD = 128
QH = 32
KVH = 4
GROUP = QH // KVH
HEADS = QH + 2 * KVH
REP = ("yl", "z")
CHIPS = ("yh", "x")
CTX = ("yh", "x", "core")
MASKED = -3e38
VMEM_BYTES = 16 * 1024 * 1024
BETWEEN = 1 << 36
MOST_VMEM = 48 * 1024 * 1024
ALL_VMEM = 60 * 1024 * 1024


def spread(rows):
    return jnp.concatenate(
        [jnp.broadcast_to(rows[g : g + 1], (2 * GROUP, HD)) for g in range(KVH)], axis=0
    )


def joint(first, second):
    pieces = []
    for g in range(KVH):
        pieces += [first[g * GROUP : (g + 1) * GROUP], second[g * GROUP : (g + 1) * GROUP]]
    return jnp.concatenate(pieces, axis=0)


def by_step(rows):
    return jnp.concatenate(
        [
            rows[(2 * g + step) * GROUP : (2 * g + step + 1) * GROUP]
            for step in range(2)
            for g in range(KVH)
        ],
        axis=0,
    )


def scored(query, keys, start, length):
    scores = jnp.concatenate(
        [
            lax.dot_general(
                query[2 * g * GROUP : 2 * (g + 1) * GROUP],
                keys[:, g * HD : (g + 1) * HD],
                (((1,), (1,)), ((), ())),
                preferred_element_type=jnp.float32,
            )
            for g in range(KVH)
        ],
        axis=0,
    ) * HD ** (-0.5)
    position = start + lax.broadcasted_iota(jnp.int32, (1, keys.shape[0]), 1)
    return jnp.where(position < length, scores, MASKED)


def weighted(rounded, values):
    return jnp.concatenate(
        [
            jnp.dot(
                rounded[2 * g * GROUP : 2 * (g + 1) * GROUP],
                values[:, g * HD : (g + 1) * HD],
                preferred_element_type=jnp.float32,
            )
            for g in range(KVH)
        ],
        axis=0,
    )


def as_row(column):
    rows = column.shape[0]
    diagonal = lax.broadcasted_iota(jnp.int32, (rows, HD), 0) == lax.broadcasted_iota(
        jnp.int32, (rows, HD), 1
    )
    return jnp.sum(jnp.where(diagonal, column, 0.0), axis=0, keepdims=True)


def pad_lanes(row):
    return jnp.concatenate([row, jnp.zeros((1, HD - row.shape[1]), row.dtype)], axis=1)


def as_column(row, rows):
    diagonal = lax.broadcasted_iota(jnp.int32, (rows, HD), 0) == lax.broadcasted_iota(
        jnp.int32, (rows, HD), 1
    )
    return jnp.sum(jnp.where(diagonal, row, 0.0), axis=1, keepdims=True)


def stage_kernel(cache, other, scratch, arrived, left):
    core = lax.axis_index("core")
    parts = arrived.shape[0] // 2
    rows = cache.shape[2] // parts
    pieces = [(kind, pl.ds(part * rows, rows)) for kind in range(2) for part in range(parts)]
    inward = [
        pltpu.make_async_copy(cache.at[1 - core, kind, block], scratch.at[kind, block], arrived.at[i])
        for i, (kind, block) in enumerate(pieces)
    ]
    outward = [
        pltpu.make_async_copy(scratch.at[kind, block], other.at[kind, block], left.at[i])
        for i, (kind, block) in enumerate(pieces)
    ]
    for copy in inward:
        copy.start()
    for first, second in zip(inward, outward):
        first.wait()
        second.start()
    for copy in outward:
        copy.wait()


def prepare_kernel(
    lengths, queries, fresh, frequency, cache, length, cosine, sine, query, new_rows, own_keys, semaphore
):
    core = lax.axis_index("core")
    copy = pltpu.make_async_copy(cache.at[core, 0], own_keys, semaphore)
    copy.start()
    length[...] = jnp.zeros_like(length) + lengths[core]
    angles = (lengths[core] + 1).astype(jnp.float32) * frequency[...]
    lane = lax.broadcasted_iota(jnp.int32, (1, HD), 1)
    cosine[...] = jnp.cos(angles)
    sine[...] = jnp.where(lane < HD // 2, -1.0, 1.0) * jnp.sin(angles)
    wide = queries[...].astype(jnp.float32)
    wide = jnp.where(core == 0, wide[0:1], wide[1:2])
    query[...] = jnp.concatenate(
        [wide[:, i * HD : (i + 1) * HD] for i in range(QH)], axis=0
    ).astype(jnp.bfloat16)
    wide = fresh[...].astype(jnp.float32)
    wide = jnp.where(core == 0, wide[0:1], wide[1:2])
    new_rows[...] = jnp.concatenate(
        [wide[:, i * HD : (i + 1) * HD] for i in range(2 * KVH)], axis=0
    ).astype(jnp.bfloat16)
    copy.wait()


def route_kernel(hidden, owners, out):
    slots = owners.shape[1]
    columns = hidden.shape[1]
    bucket_rows = columns // slots
    column = lax.broadcasted_iota(jnp.int32, (slots, columns), 1)
    first = lax.broadcasted_iota(jnp.int32, (slots, columns), 0) * bucket_rows
    inside = (column >= first) & (column < first + bucket_rows)
    owner = jnp.sum(
        jnp.where(inside, as_column(pad_lanes(owners[...].astype(jnp.float32)), slots), 0.0),
        axis=0,
        keepdims=True,
    )
    chosen = owner == lax.broadcasted_iota(jnp.int32, (slots, columns), 0).astype(jnp.float32)
    row = lax.broadcasted_iota(jnp.int32, (columns, HD), 0)
    lane = lax.broadcasted_iota(jnp.int32, (columns, HD), 1)
    bucket = jnp.floor((row.astype(jnp.float32) + 0.5) * (1.0 / bucket_rows)).astype(jnp.int32)
    fold = row == lane + bucket * bucket_rows
    fold = jnp.where(fold, 1.0, 0.0).astype(jnp.bfloat16)
    for core in range(2):
        kept = jnp.where(chosen, hidden[core : core + 1].astype(jnp.float32), 0.0)
        folded = jnp.dot(kept.astype(jnp.bfloat16), fold, preferred_element_type=jnp.float32)
        out[core * slots : (core + 1) * slots] = jnp.broadcast_to(
            folded[:, None, :], (slots, 2, HD)
        )


def project_kernel(hidden, own_rows, other_rows, out, rows, wide):
    core = lax.axis_index("core")
    bucket_rows = own_rows.shape[0]
    slots = out.shape[0]
    rows[...] = jnp.zeros_like(rows)
    rows[0:bucket_rows] = own_rows[...]
    rows[16 : 16 + bucket_rows] = other_rows[...]
    received = hidden[:, 0, :].astype(jnp.bfloat16)
    own = jnp.where(core == 0, received[:slots], received[slots:])[:, :16]
    other = jnp.where(core == 0, received[slots:], received[:slots])[:, :16]
    both = jnp.concatenate([own, other], axis=1)
    step = 8
    for start in range(0, out.shape[1], step):
        block = jnp.dot(
            both,
            rows[:, start * HD : (start + step) * HD],
            preferred_element_type=jnp.float32,
        )
        for i in range(step):
            wide[:, start + i, :] = block[:, i * HD : (i + 1) * HD]
    out[...] = wide[...].astype(jnp.bfloat16)


def reduce_kernel(received, out):
    total = received[0].astype(jnp.float32)
    for i in range(1, received.shape[0]):
        total += received[i].astype(jnp.float32)
    total = total.astype(jnp.bfloat16)
    for i in range(out.shape[0]):
        out[i] = total


def steps_kernel(
    length, shares, cosine, sine, first_query, fresh, cache, other, own_keys, out, own_values,
    held, kept, semaphore,
):
    core = lax.axis_index("core")
    chip = lax.axis_index(CHIPS)
    positions = own_keys.shape[0]
    copy = pltpu.make_async_copy(cache.at[core, 1], own_values, semaphore)
    copy.start()
    rows = 2 * QH

    @pl.when(chip >= 0)
    def _():
        projected = shares[0].astype(jnp.float32)
        for i in range(1, shares.shape[0]):
            projected += shares[i].astype(jnp.float32)
        turned = projected[: QH + KVH]
        turned = turned * cosine[...] + pltpu.roll(turned, HD // 2, 1) * sine[...]
        second = jnp.concatenate([turned[QH:], projected[QH + KVH :]], axis=0)
        query = joint(first_query[...].astype(jnp.float32), turned[:QH]).astype(jnp.bfloat16)
        limit = length[:, 0:1]
        parts = [
            scored(query, other.at[0], (chip * 2 + 1 - core) * positions, limit),
            scored(query, own_keys, (chip * 2 + core) * positions, limit),
        ]

        wide = query.astype(jnp.float32)
        rows = 2 * QH
        step = (lax.broadcasted_iota(jnp.int32, (rows, 1), 0) // GROUP) % 2
        earlier = fresh[...].astype(jnp.float32)
        later = second.astype(jnp.bfloat16).astype(jnp.float32)
        extras = []
        for token, counted in ((earlier, step >= 0), (later, step == 1)):
            score = jnp.sum(wide * spread(token[:KVH]), axis=1, keepdims=True) * HD ** (-0.5)
            extras.append(jnp.where(counted & (chip == 0), score, MASKED))

        biggest = jnp.maximum(extras[0], extras[1])
        for part in parts:
            biggest = jnp.maximum(biggest, jnp.max(part, axis=1, keepdims=True))
        total = jnp.zeros((rows, 1), jnp.float32)
        summed = jnp.zeros((rows, HD), jnp.float32)
        for score, token in zip(extras, (earlier, later)):
            exponential = jnp.where(score > 0.5 * MASKED, jnp.exp(score - biggest), 0.0)
            total += exponential
            summed += exponential.astype(jnp.bfloat16).astype(jnp.float32) * spread(token[KVH:])
        rounded = []
        for part in parts:
            exponentials = jnp.where(part > 0.5 * MASKED, jnp.exp(part - biggest), 0.0)
            total += jnp.sum(exponentials, axis=1, keepdims=True)
            rounded.append(exponentials.astype(jnp.bfloat16))
        summed += weighted(rounded[0], other.at[1])
        used = total > 0.0
        safe = jnp.where(used, total, 1.0)
        held[0] = summed
        held[1] = jnp.broadcast_to(1.0 / safe, (rows, HD))
        weights = as_row(by_step(jnp.where(used, biggest + jnp.log(safe), MASKED)))
        high = weights.astype(jnp.bfloat16).astype(jnp.float32)
        middle = (weights - high).astype(jnp.bfloat16).astype(jnp.float32)
        low = weights - high - middle
        tail = jnp.concatenate([second, high, middle, low, jnp.zeros((5, HD), jnp.float32)], axis=0)
        tail = tail.astype(jnp.bfloat16)
        for i in range(out.shape[0]):
            out[i, rows:] = tail
        kept[...] = rounded[1]

    @pl.when(chip >= 0)
    def _():
        copy.wait()
        attended = (held[0] + weighted(kept[...], own_values)) * held[1]
        attended = by_step(attended).astype(jnp.bfloat16)
        for i in range(out.shape[0]):
            out[i, :rows] = attended


def flat(rows):
    return jnp.concatenate([rows[i : i + 1] for i in range(rows.shape[0])], axis=1)


def combine_kernel(shares, attended, made):
    count = shares.shape[0] // 2
    heads = 2 * QH
    fresh = []
    for core in range(2):
        weights = []
        for i in range(count):
            share = shares[2 * i + core]
            pieces = share[heads + 2 * KVH :].astype(jnp.float32)
            weights.append(as_column(pieces[0:1] + pieces[1:2] + pieces[2:3], heads))
        biggest = weights[0]
        for weight in weights[1:]:
            biggest = jnp.maximum(biggest, weight)
        total = jnp.zeros((heads, 1), jnp.float32)
        summed = jnp.zeros((heads, HD), jnp.float32)
        for i in range(count):
            scale = jnp.exp(weights[i] - biggest)
            total += scale
            summed += scale * shares[2 * i + core, :heads].astype(jnp.float32)
        merged = summed / total
        attended[core] = jnp.concatenate([flat(merged[:QH]), flat(merged[QH:])], axis=0).astype(
            jnp.bfloat16
        )
        fresh.append(flat(shares[core, heads : heads + 2 * KVH].astype(jnp.float32)))
    made[...] = jnp.concatenate(fresh, axis=0).astype(jnp.bfloat16)


def kernel_call(
    kernel, out_shape, name, operands, spaces="", scratch=(), limit=VMEM_BYTES, work=0
):
    kinds = {"v": pltpu.VMEM, "s": pltpu.SMEM, "h": pltpu.HBM}
    spaces = spaces or "v" * len(operands)
    moved = sum(one.size * one.dtype.itemsize for one in (*operands, *out_shape))
    return pl.pallas_call(
        kernel,
        in_specs=[pl.BlockSpec(memory_space=kinds[one]) for one in spaces],
        out_specs=[pl.BlockSpec(memory_space=pltpu.VMEM)] * len(out_shape),
        out_shape=out_shape,
        scratch_shapes=scratch,
        compiler_params=pltpu.CompilerParams(vmem_limit_bytes=limit),
        cost_estimate=pl.CostEstimate(flops=work, bytes_accessed=moved, transcendentals=0),
        name=name,
    )(*operands)


def swap(value):
    return lax.ppermute(value, "core", [(0, 1), (1, 0)])


def local(q_first, kv_first, hidden_next, lengths, owners, sectioned, kv_cache):
    rep_size = lax.axis_size(REP)
    chips = lax.axis_size(CHIPS)
    core = lax.axis_index("core")
    bf16, f32 = jnp.bfloat16, jnp.float32
    shape = jax.ShapeDtypeStruct
    _, _, positions, columns = kv_cache.shape

    (by_slot,) = kernel_call(
        route_kernel,
        (shape((2 * rep_size, 2, HD), f32),),
        "route_hidden",
        (hidden_next, owners),
        limit=ALL_VMEM,
    )
    by_slot, sectioned, kv_cache = lax.optimization_barrier((by_slot, sectioned, kv_cache))
    hidden = lax.all_to_all(by_slot, ("core",) + REP, 0, 0, tiled=True)
    other_rows = swap(sectioned[0])
    staged = pl.pallas_call(
        stage_kernel,
        in_specs=[pl.BlockSpec(memory_space=pltpu.HBM)],
        out_specs=pl.BlockSpec(memory_space=pltpu.HBM),
        out_shape=shape(kv_cache.shape[1:], bf16),
        scratch_shapes=[
            pltpu.VMEM(kv_cache.shape[1:], bf16),
            pltpu.SemaphoreType.DMA((4,)),
            pltpu.SemaphoreType.DMA((4,)),
        ],
        compiler_params=pltpu.CompilerParams(vmem_limit_bytes=ALL_VMEM),
        cost_estimate=pl.CostEstimate(flops=0, bytes_accessed=8 * positions * columns, transcendentals=0),
        name="stage_cache",
    )(kv_cache)
    hidden, other_rows, _ = lax.optimization_barrier((hidden, other_rows, staged))
    (partial_sum,) = kernel_call(
        project_kernel,
        (shape((rep_size, HEADS, HD), bf16),),
        "project",
        (hidden, sectioned[0], other_rows),
        scratch=[
            pltpu.VMEM((32, HEADS * HD), bf16),
            pltpu.VMEM((rep_size, HEADS, HD), f32),
        ],
    )
    partial_sum, staged = lax.optimization_barrier((partial_sum, staged))
    received = lax.all_to_all(partial_sum, REP, 0, 0, tiled=True)
    other_cache = swap(staged)

    halved = np.float32(1000000.0) ** (-(np.arange(HD // 2, dtype=np.float32) * 2.0 / HD))
    frequency = jnp.asarray(np.concatenate([halved, halved])[None], f32)
    length, cosine, sine, query, fresh, own_keys = kernel_call(
        prepare_kernel,
        (
            shape((1, HD), jnp.int32),
            shape((1, HD), f32),
            shape((1, HD), f32),
            shape((QH, HD), bf16),
            shape((2 * KVH, HD), bf16),
            shape((positions, columns), bf16),
        ),
        "prepare_rows",
        (lengths, q_first, kv_first, frequency, kv_cache),
        spaces="svvvh",
        scratch=[pltpu.SemaphoreType.DMA],
        limit=52 * 1024 * 1024,
        work=BETWEEN,
    )
    received, length = lax.optimization_barrier((received, length))
    (reduced,) = kernel_call(
        reduce_kernel, (shape((chips, HEADS, HD), bf16),), "sum_over_replicas", (received,)
    )
    shares = lax.all_to_all(reduced, CHIPS, 0, 0, tiled=True)
    (payload,) = kernel_call(
        steps_kernel,
        (shape((2 * chips, 80, HD), bf16),),
        "both_steps",
        (length, shares, cosine, sine, query, fresh, kv_cache, other_cache, own_keys),
        spaces="vvvvvvhvv",
        scratch=[
            pltpu.VMEM((positions, columns), bf16),
            pltpu.VMEM((2, 2 * QH, HD), f32),
            pltpu.VMEM((2 * QH, positions), bf16),
            pltpu.SemaphoreType.DMA,
        ],
        limit=MOST_VMEM,
    )
    gathered = lax.all_to_all(payload, CTX, 0, 0, tiled=True)
    attended, made = kernel_call(
        combine_kernel,
        (shape((2, 2, QH * HD), bf16), shape((2, 2 * KVH * HD), bf16)),
        "combine",
        (gathered,),
    )
    return attended, made


def solution(mesh):
    fine = Mesh(mesh.devices.reshape(4, 8, 2, 4, 2), ("yl", "z", "yh", "x", "core"))
    placed = (
        P(REP, None),
        P(REP, None),
        P(REP, CTX),
        P(REP),
        P(CTX, None),
        P(REP, CTX, None),
        P(REP, None, CTX, None),
    )
    return jax.shard_map(
        local,
        mesh=fine,
        in_specs=placed,
        out_specs=(P(REP, None, None), P(REP, None)),
        check_vma=False,
    )
```

```python
import jax
import jax.numpy as jnp
import numpy as np
from jax import lax
from jax.experimental import pallas as pl
from jax.experimental.pallas import tpu as pltpu
from jax.sharding import Mesh, PartitionSpec as P

HD = 128
QH = 32
KVH = 4
GROUP = QH // KVH
HEADS = QH + 2 * KVH
REP = ("yl", "z")
CHIPS = ("yh", "x")
CTX = ("yh", "x", "core")
MASKED = -3e38
VMEM_BYTES = 16 * 1024 * 1024
BETWEEN = 1 << 36
MOST_VMEM = 48 * 1024 * 1024
ALL_VMEM = 60 * 1024 * 1024


def spread(rows):
    return jnp.concatenate(
        [jnp.broadcast_to(rows[g : g + 1], (2 * GROUP, HD)) for g in range(KVH)], axis=0
    )


def joint(first, second):
    pieces = []
    for g in range(KVH):
        pieces += [first[g * GROUP : (g + 1) * GROUP], second[g * GROUP : (g + 1) * GROUP]]
    return jnp.concatenate(pieces, axis=0)


def by_step(rows):
    return jnp.concatenate(
        [
            rows[(2 * g + step) * GROUP : (2 * g + step + 1) * GROUP]
            for step in range(2)
            for g in range(KVH)
        ],
        axis=0,
    )


def scored(query, keys, start, length):
    scores = jnp.concatenate(
        [
            lax.dot_general(
                query[2 * g * GROUP : 2 * (g + 1) * GROUP],
                keys[:, g * HD : (g + 1) * HD],
                (((1,), (1,)), ((), ())),
                preferred_element_type=jnp.float32,
            )
            for g in range(KVH)
        ],
        axis=0,
    ) * HD ** (-0.5)
    position = start + lax.broadcasted_iota(jnp.int32, (1, keys.shape[0]), 1)
    return jnp.where(position < length, scores, MASKED)


def weighted(rounded, values):
    return jnp.concatenate(
        [
            jnp.dot(
                rounded[2 * g * GROUP : 2 * (g + 1) * GROUP],
                values[:, g * HD : (g + 1) * HD],
                preferred_element_type=jnp.float32,
            )
            for g in range(KVH)
        ],
        axis=0,
    )


def as_row(column):
    rows = column.shape[0]
    diagonal = lax.broadcasted_iota(jnp.int32, (rows, HD), 0) == lax.broadcasted_iota(
        jnp.int32, (rows, HD), 1
    )
    return jnp.sum(jnp.where(diagonal, column, 0.0), axis=0, keepdims=True)


def pad_lanes(row):
    return jnp.concatenate([row, jnp.zeros((1, HD - row.shape[1]), row.dtype)], axis=1)


def as_column(row, rows):
    diagonal = lax.broadcasted_iota(jnp.int32, (rows, HD), 0) == lax.broadcasted_iota(
        jnp.int32, (rows, HD), 1
    )
    return jnp.sum(jnp.where(diagonal, row, 0.0), axis=1, keepdims=True)


def stage_kernel(cache, other, scratch, arrived, left):
    core = lax.axis_index("core")
    parts = arrived.shape[0] // 2
    rows = cache.shape[2] // parts
    pieces = [(kind, pl.ds(part * rows, rows)) for kind in range(2) for part in range(parts)]
    inward = [
        pltpu.make_async_copy(cache.at[1 - core, kind, block], scratch.at[kind, block], arrived.at[i])
        for i, (kind, block) in enumerate(pieces)
    ]
    outward = [
        pltpu.make_async_copy(scratch.at[kind, block], other.at[kind, block], left.at[i])
        for i, (kind, block) in enumerate(pieces)
    ]
    for copy in inward:
        copy.start()
    for first, second in zip(inward, outward):
        first.wait()
        second.start()
    for copy in outward:
        copy.wait()


def prepare_kernel(
    lengths, queries, fresh, frequency, cache, length, cosine, sine, query, new_rows, own_keys, semaphore
):
    core = lax.axis_index("core")
    copy = pltpu.make_async_copy(cache.at[core, 0], own_keys, semaphore)
    copy.start()
    length[...] = jnp.zeros_like(length) + lengths[core]
    angles = (lengths[core] + 1).astype(jnp.float32) * frequency[...]
    lane = lax.broadcasted_iota(jnp.int32, (1, HD), 1)
    cosine[...] = jnp.cos(angles)
    sine[...] = jnp.where(lane < HD // 2, -1.0, 1.0) * jnp.sin(angles)
    wide = queries[...].astype(jnp.float32)
    wide = jnp.where(core == 0, wide[0:1], wide[1:2])
    query[...] = jnp.concatenate(
        [wide[:, i * HD : (i + 1) * HD] for i in range(QH)], axis=0
    ).astype(jnp.bfloat16)
    wide = fresh[...].astype(jnp.float32)
    wide = jnp.where(core == 0, wide[0:1], wide[1:2])
    new_rows[...] = jnp.concatenate(
        [wide[:, i * HD : (i + 1) * HD] for i in range(2 * KVH)], axis=0
    ).astype(jnp.bfloat16)
    copy.wait()


def route_kernel(hidden, owners, out):
    slots = owners.shape[1]
    columns = hidden.shape[1]
    bucket_rows = columns // slots
    column = lax.broadcasted_iota(jnp.int32, (slots, columns), 1)
    first = lax.broadcasted_iota(jnp.int32, (slots, columns), 0) * bucket_rows
    inside = (column >= first) & (column < first + bucket_rows)
    owner = jnp.sum(
        jnp.where(inside, as_column(pad_lanes(owners[...].astype(jnp.float32)), slots), 0.0),
        axis=0,
        keepdims=True,
    )
    chosen = owner == lax.broadcasted_iota(jnp.int32, (slots, columns), 0).astype(jnp.float32)
    row = lax.broadcasted_iota(jnp.int32, (columns, HD), 0)
    lane = lax.broadcasted_iota(jnp.int32, (columns, HD), 1)
    bucket = jnp.floor((row.astype(jnp.float32) + 0.5) * (1.0 / bucket_rows)).astype(jnp.int32)
    fold = row == lane + bucket * bucket_rows
    fold = jnp.where(fold, 1.0, 0.0).astype(jnp.bfloat16)
    for core in range(2):
        kept = jnp.where(chosen, hidden[core : core + 1].astype(jnp.float32), 0.0)
        folded = jnp.dot(kept.astype(jnp.bfloat16), fold, preferred_element_type=jnp.float32)
        out[core * slots : (core + 1) * slots] = jnp.broadcast_to(
            folded[:, None, :], (slots, 2, HD)
        )


def project_kernel(hidden, own_rows, other_rows, out, rows, wide):
    core = lax.axis_index("core")
    bucket_rows = own_rows.shape[0]
    slots = out.shape[0]
    rows[...] = jnp.zeros_like(rows)
    rows[0:bucket_rows] = own_rows[...]
    rows[16 : 16 + bucket_rows] = other_rows[...]
    received = hidden[:, 0, :].astype(jnp.bfloat16)
    own = jnp.where(core == 0, received[:slots], received[slots:])[:, :16]
    other = jnp.where(core == 0, received[slots:], received[:slots])[:, :16]
    both = jnp.concatenate([own, other], axis=1)
    step = 8
    for start in range(0, out.shape[1], step):
        block = jnp.dot(
            both,
            rows[:, start * HD : (start + step) * HD],
            preferred_element_type=jnp.float32,
        )
        for i in range(step):
            wide[:, start + i, :] = block[:, i * HD : (i + 1) * HD]
    out[...] = wide[...].astype(jnp.bfloat16)


def reduce_kernel(received, out):
    total = received[0].astype(jnp.float32)
    for i in range(1, received.shape[0]):
        total += received[i].astype(jnp.float32)
    total = total.astype(jnp.bfloat16)
    for i in range(out.shape[0]):
        out[i] = total


def steps_kernel(
    length, shares, cosine, sine, first_query, fresh, cache, other, own_keys, out, made,
    own_values, held, kept, semaphore,
):
    core = lax.axis_index("core")
    chip = lax.axis_index(CHIPS)
    positions = own_keys.shape[0]
    copy = pltpu.make_async_copy(cache.at[core, 1], own_values, semaphore)
    copy.start()
    rows = 2 * QH

    @pl.when(chip >= 0)
    def _():
        projected = shares[0].astype(jnp.float32)
        for i in range(1, shares.shape[0]):
            projected += shares[i].astype(jnp.float32)
        turned = projected[: QH + KVH]
        turned = turned * cosine[...] + pltpu.roll(turned, HD // 2, 1) * sine[...]
        second = jnp.concatenate([turned[QH:], projected[QH + KVH :]], axis=0)
        query = joint(first_query[...].astype(jnp.float32), turned[:QH]).astype(jnp.bfloat16)
        limit = length[:, 0:1]
        parts = [
            scored(query, other.at[0], (chip * 2 + 1 - core) * positions, limit),
            scored(query, own_keys, (chip * 2 + core) * positions, limit),
        ]

        wide = query.astype(jnp.float32)
        rows = 2 * QH
        step = (lax.broadcasted_iota(jnp.int32, (rows, 1), 0) // GROUP) % 2
        earlier = fresh[...].astype(jnp.float32)
        later = second.astype(jnp.bfloat16).astype(jnp.float32)
        extras = []
        for token, counted in ((earlier, step >= 0), (later, step == 1)):
            score = jnp.sum(wide * spread(token[:KVH]), axis=1, keepdims=True) * HD ** (-0.5)
            extras.append(jnp.where(counted & (chip == 0), score, MASKED))

        biggest = jnp.maximum(extras[0], extras[1])
        for part in parts:
            biggest = jnp.maximum(biggest, jnp.max(part, axis=1, keepdims=True))
        total = jnp.zeros((rows, 1), jnp.float32)
        summed = jnp.zeros((rows, HD), jnp.float32)
        for score, token in zip(extras, (earlier, later)):
            exponential = jnp.where(score > 0.5 * MASKED, jnp.exp(score - biggest), 0.0)
            total += exponential
            summed += exponential.astype(jnp.bfloat16).astype(jnp.float32) * spread(token[KVH:])
        rounded = []
        for part in parts:
            exponentials = jnp.where(part > 0.5 * MASKED, jnp.exp(part - biggest), 0.0)
            total += jnp.sum(exponentials, axis=1, keepdims=True)
            rounded.append(exponentials.astype(jnp.bfloat16))
        summed += weighted(rounded[0], other.at[1])
        used = total > 0.0
        safe = jnp.where(used, total, 1.0)
        held[0] = summed
        held[1] = jnp.broadcast_to(1.0 / safe, (rows, HD))
        weights = as_row(by_step(jnp.where(used, biggest + jnp.log(safe), MASKED)))
        high = weights.astype(jnp.bfloat16).astype(jnp.float32)
        middle = (weights - high).astype(jnp.bfloat16).astype(jnp.float32)
        low = weights - high - middle
        made[...] = second.astype(jnp.bfloat16)
        tail = jnp.concatenate([high, middle, low, jnp.zeros((5, HD), jnp.float32)], axis=0)
        tail = tail.astype(jnp.bfloat16)
        for i in range(out.shape[0]):
            out[i, rows:] = tail
        kept[...] = rounded[1]

    @pl.when(chip >= 0)
    def _():
        copy.wait()
        attended = (held[0] + weighted(kept[...], own_values)) * held[1]
        attended = by_step(attended).astype(jnp.bfloat16)
        for i in range(out.shape[0]):
            out[i, :rows] = attended


def flat(rows):
    return jnp.concatenate([rows[i : i + 1] for i in range(rows.shape[0])], axis=1)


def combine_kernel(shares, made, out):
    rows = 2 * QH
    weights = []
    for i in range(shares.shape[0]):
        pieces = shares[i, rows:].astype(jnp.float32)
        weights.append(as_column(pieces[0:1] + pieces[1:2] + pieces[2:3], rows))
    biggest = weights[0]
    for weight in weights[1:]:
        biggest = jnp.maximum(biggest, weight)
    total = jnp.zeros((rows, 1), jnp.float32)
    summed = jnp.zeros((rows, HD), jnp.float32)
    for i, weight in enumerate(weights):
        scale = jnp.exp(weight - biggest)
        total += scale
        summed += scale * shares[i, :rows].astype(jnp.float32)
    out[:rows] = (summed / total).astype(jnp.bfloat16)
    out[rows:] = made[...]


def assemble_kernel(mine, theirs, attended, made):
    core = lax.axis_index("core")
    own, other = mine[...].astype(jnp.float32), theirs[...].astype(jnp.float32)
    fresh = []
    for rows in (jnp.where(core == 0, own, other), jnp.where(core == 0, other, own)):
        attended[len(fresh)] = jnp.concatenate(
            [flat(rows[:QH]), flat(rows[QH : 2 * QH])], axis=0
        ).astype(jnp.bfloat16)
        fresh.append(flat(rows[2 * QH :]))
    made[...] = jnp.concatenate(fresh, axis=0).astype(jnp.bfloat16)


def kernel_call(
    kernel, out_shape, name, operands, spaces="", scratch=(), limit=VMEM_BYTES, work=0
):
    kinds = {"v": pltpu.VMEM, "s": pltpu.SMEM, "h": pltpu.HBM}
    spaces = spaces or "v" * len(operands)
    moved = sum(one.size * one.dtype.itemsize for one in (*operands, *out_shape))
    return pl.pallas_call(
        kernel,
        in_specs=[pl.BlockSpec(memory_space=kinds[one]) for one in spaces],
        out_specs=[pl.BlockSpec(memory_space=pltpu.VMEM)] * len(out_shape),
        out_shape=out_shape,
        scratch_shapes=scratch,
        compiler_params=pltpu.CompilerParams(vmem_limit_bytes=limit),
        cost_estimate=pl.CostEstimate(flops=work, bytes_accessed=moved, transcendentals=0),
        name=name,
    )(*operands)


def swap(value):
    return lax.ppermute(value, "core", [(0, 1), (1, 0)])


def local(q_first, kv_first, hidden_next, lengths, owners, sectioned, kv_cache):
    rep_size = lax.axis_size(REP)
    chips = lax.axis_size(CHIPS)
    core = lax.axis_index("core")
    bf16, f32 = jnp.bfloat16, jnp.float32
    shape = jax.ShapeDtypeStruct
    _, _, positions, columns = kv_cache.shape

    (by_slot,) = kernel_call(
        route_kernel,
        (shape((2 * rep_size, 2, HD), f32),),
        "route_hidden",
        (hidden_next, owners),
        limit=ALL_VMEM,
    )
    by_slot, sectioned, kv_cache = lax.optimization_barrier((by_slot, sectioned, kv_cache))
    hidden = lax.all_to_all(by_slot, ("core",) + REP, 0, 0, tiled=True)
    other_rows = swap(sectioned[0])
    staged = pl.pallas_call(
        stage_kernel,
        in_specs=[pl.BlockSpec(memory_space=pltpu.HBM)],
        out_specs=pl.BlockSpec(memory_space=pltpu.HBM),
        out_shape=shape(kv_cache.shape[1:], bf16),
        scratch_shapes=[
            pltpu.VMEM(kv_cache.shape[1:], bf16),
            pltpu.SemaphoreType.DMA((4,)),
            pltpu.SemaphoreType.DMA((4,)),
        ],
        compiler_params=pltpu.CompilerParams(vmem_limit_bytes=ALL_VMEM),
        cost_estimate=pl.CostEstimate(flops=0, bytes_accessed=8 * positions * columns, transcendentals=0),
        name="stage_cache",
    )(kv_cache)
    hidden, other_rows, _ = lax.optimization_barrier((hidden, other_rows, staged))
    (partial_sum,) = kernel_call(
        project_kernel,
        (shape((rep_size, HEADS, HD), bf16),),
        "project",
        (hidden, sectioned[0], other_rows),
        scratch=[
            pltpu.VMEM((32, HEADS * HD), bf16),
            pltpu.VMEM((rep_size, HEADS, HD), f32),
        ],
    )
    partial_sum, staged = lax.optimization_barrier((partial_sum, staged))
    received = lax.all_to_all(partial_sum, REP, 0, 0, tiled=True)
    other_cache = swap(staged)

    halved = np.float32(1000000.0) ** (-(np.arange(HD // 2, dtype=np.float32) * 2.0 / HD))
    frequency = jnp.asarray(np.concatenate([halved, halved])[None], f32)
    length, cosine, sine, query, fresh, own_keys = kernel_call(
        prepare_kernel,
        (
            shape((1, HD), jnp.int32),
            shape((1, HD), f32),
            shape((1, HD), f32),
            shape((QH, HD), bf16),
            shape((2 * KVH, HD), bf16),
            shape((positions, columns), bf16),
        ),
        "prepare_rows",
        (lengths, q_first, kv_first, frequency, kv_cache),
        spaces="svvvh",
        scratch=[pltpu.SemaphoreType.DMA],
        limit=52 * 1024 * 1024,
        work=BETWEEN,
    )
    received, length = lax.optimization_barrier((received, length))
    (reduced,) = kernel_call(
        reduce_kernel, (shape((chips, HEADS, HD), bf16),), "sum_over_replicas", (received,)
    )
    shares = lax.all_to_all(reduced, CHIPS, 0, 0, tiled=True)
    payload, made = kernel_call(
        steps_kernel,
        (shape((chips, 2 * QH + 8, HD), bf16), shape((2 * KVH, HD), bf16)),
        "both_steps",
        (length, shares, cosine, sine, query, fresh, kv_cache, other_cache, own_keys),
        spaces="vvvvvvhvv",
        scratch=[
            pltpu.VMEM((positions, columns), bf16),
            pltpu.VMEM((2, 2 * QH, HD), f32),
            pltpu.VMEM((2 * QH, positions), bf16),
            pltpu.SemaphoreType.DMA,
        ],
        limit=MOST_VMEM,
    )
    gathered = lax.all_to_all(payload, CHIPS, 0, 0, tiled=True)
    (mine,) = kernel_call(
        combine_kernel,
        (shape((2 * QH + 2 * KVH, HD), bf16),),
        "combine",
        (gathered, made),
    )
    attended, made = kernel_call(
        assemble_kernel,
        (shape((2, 2, QH * HD), bf16), shape((2, 2 * KVH * HD), bf16)),
        "assemble",
        (mine, swap(mine)),
    )
    return attended, made


def solution(mesh):
    fine = Mesh(mesh.devices.reshape(4, 8, 2, 4, 2), ("yl", "z", "yh", "x", "core"))
    placed = (
        P(REP, None),
        P(REP, None),
        P(REP, CTX),
        P(REP),
        P(CTX, None),
        P(REP, CTX, None),
        P(REP, None, CTX, None),
    )
    return jax.shard_map(
        local,
        mesh=fine,
        in_specs=placed,
        out_specs=(P(REP, None, None), P(REP, None)),
        check_vma=False,
    )
```

```python
import jax
import jax.numpy as jnp
import numpy as np
from jax import lax
from jax.experimental import pallas as pl
from jax.experimental.pallas import tpu as pltpu
from jax.sharding import Mesh, PartitionSpec as P

HD = 128
QH = 32
KVH = 4
GROUP = QH // KVH
HEADS = QH + 2 * KVH
REP = ("yp", "yq", "z")
FOLD = ("yp", "z")
CHIPS = ("yh", "x")
CTX = ("yh", "x", "core")
MASKED = -3e38
VMEM_BYTES = 16 * 1024 * 1024
BETWEEN = 1 << 36
MOST_VMEM = 48 * 1024 * 1024
ALL_VMEM = 60 * 1024 * 1024


def spread(rows):
    return jnp.concatenate(
        [jnp.broadcast_to(rows[g : g + 1], (2 * GROUP, HD)) for g in range(KVH)], axis=0
    )


def joint(first, second):
    pieces = []
    for g in range(KVH):
        pieces += [first[g * GROUP : (g + 1) * GROUP], second[g * GROUP : (g + 1) * GROUP]]
    return jnp.concatenate(pieces, axis=0)


def by_step(rows):
    return jnp.concatenate(
        [
            rows[(2 * g + step) * GROUP : (2 * g + step + 1) * GROUP]
            for step in range(2)
            for g in range(KVH)
        ],
        axis=0,
    )


def scored(query, keys, start, length):
    scores = jnp.concatenate(
        [
            lax.dot_general(
                query[2 * g * GROUP : 2 * (g + 1) * GROUP],
                keys[:, g * HD : (g + 1) * HD],
                (((1,), (1,)), ((), ())),
                preferred_element_type=jnp.float32,
            )
            for g in range(KVH)
        ],
        axis=0,
    ) * HD ** (-0.5)
    position = start + lax.broadcasted_iota(jnp.int32, (1, keys.shape[0]), 1)
    return jnp.where(position < length, scores, MASKED)


def weighted(rounded, values):
    return jnp.concatenate(
        [
            jnp.dot(
                rounded[2 * g * GROUP : 2 * (g + 1) * GROUP],
                values[:, g * HD : (g + 1) * HD],
                preferred_element_type=jnp.float32,
            )
            for g in range(KVH)
        ],
        axis=0,
    )


def as_row(column):
    rows = column.shape[0]
    diagonal = lax.broadcasted_iota(jnp.int32, (rows, HD), 0) == lax.broadcasted_iota(
        jnp.int32, (rows, HD), 1
    )
    return jnp.sum(jnp.where(diagonal, column, 0.0), axis=0, keepdims=True)


def pad_lanes(row):
    return jnp.concatenate([row, jnp.zeros((1, HD - row.shape[1]), row.dtype)], axis=1)


def as_column(row, rows):
    diagonal = lax.broadcasted_iota(jnp.int32, (rows, HD), 0) == lax.broadcasted_iota(
        jnp.int32, (rows, HD), 1
    )
    return jnp.sum(jnp.where(diagonal, row, 0.0), axis=1, keepdims=True)


def fetch_kernel(cache, own_keys, other, scratch, arrived, left, semaphore):
    core = lax.axis_index("core")
    parts = arrived.shape[0] // 2
    rows = cache.shape[2] // parts
    pieces = [(kind, pl.ds(part * rows, rows)) for kind in range(2) for part in range(parts)]
    inward = [
        pltpu.make_async_copy(cache.at[1 - core, kind, block], scratch.at[kind, block], arrived.at[i])
        for i, (kind, block) in enumerate(pieces)
    ]
    outward = [
        pltpu.make_async_copy(scratch.at[kind, block], other.at[kind, block], left.at[i])
        for i, (kind, block) in enumerate(pieces)
    ]
    own = pltpu.make_async_copy(cache.at[core, 0], own_keys, semaphore)
    for copy in (*inward, own):
        copy.start()
    for first, second in zip(inward, outward):
        first.wait()
        second.start()
    own.wait()
    for copy in outward:
        copy.wait()


def prepare_kernel(lengths, queries, fresh, frequency, length, cosine, sine, query, new_rows):
    core = lax.axis_index("core")
    length[...] = jnp.zeros_like(length) + lengths[core]
    angles = (lengths[core] + 1).astype(jnp.float32) * frequency[...]
    lane = lax.broadcasted_iota(jnp.int32, (1, HD), 1)
    cosine[...] = jnp.cos(angles)
    sine[...] = jnp.where(lane < HD // 2, -1.0, 1.0) * jnp.sin(angles)
    wide = queries[...].astype(jnp.float32)
    wide = jnp.where(core == 0, wide[0:1], wide[1:2])
    query[...] = jnp.concatenate(
        [wide[:, i * HD : (i + 1) * HD] for i in range(QH)], axis=0
    ).astype(jnp.bfloat16)
    wide = fresh[...].astype(jnp.float32)
    wide = jnp.where(core == 0, wide[0:1], wide[1:2])
    new_rows[...] = jnp.concatenate(
        [wide[:, i * HD : (i + 1) * HD] for i in range(2 * KVH)], axis=0
    ).astype(jnp.bfloat16)


def route_kernel(hidden, owners, out):
    slots = owners.shape[1]
    columns = hidden.shape[1]
    bucket_rows = columns // slots
    column = lax.broadcasted_iota(jnp.int32, (slots, columns), 1)
    first = lax.broadcasted_iota(jnp.int32, (slots, columns), 0) * bucket_rows
    inside = (column >= first) & (column < first + bucket_rows)
    owner = jnp.sum(
        jnp.where(inside, as_column(pad_lanes(owners[...].astype(jnp.float32)), slots), 0.0),
        axis=0,
        keepdims=True,
    )
    chosen = owner == lax.broadcasted_iota(jnp.int32, (slots, columns), 0).astype(jnp.float32)
    row = lax.broadcasted_iota(jnp.int32, (columns, HD), 0)
    lane = lax.broadcasted_iota(jnp.int32, (columns, HD), 1)
    bucket = jnp.floor((row.astype(jnp.float32) + 0.5) * (1.0 / bucket_rows)).astype(jnp.int32)
    fold = row == lane + bucket * bucket_rows
    fold = jnp.where(fold, 1.0, 0.0).astype(jnp.bfloat16)
    for core in range(2):
        kept = jnp.where(chosen, hidden[core : core + 1].astype(jnp.float32), 0.0)
        folded = jnp.dot(kept.astype(jnp.bfloat16), fold, preferred_element_type=jnp.float32)
        column_size = slots // 4
        for outer in range(2):
            first = (2 * core + outer) * column_size
            for pair in range(2):
                block = (2 * outer + pair) * column_size
                out[first : first + column_size, pair, :] = folded[block : block + column_size]


def pack_kernel(own_rows, pair_rows, near_rows):
    bucket_rows = own_rows.shape[0]
    near_rows[...] = jnp.zeros_like(near_rows)
    near_rows[0:bucket_rows] = own_rows[...]
    near_rows[16 : 16 + bucket_rows] = pair_rows[...]


def project_kernel(hidden, near_rows, far_rows, far_pair, out, rows, wide):
    core = lax.axis_index("core")
    side = lax.axis_index("yq")
    bucket_rows = far_rows.shape[0]
    slots = out.shape[0]
    rows[...] = jnp.zeros_like(rows)
    rows[0:bucket_rows] = far_rows[...]
    rows[16 : 16 + bucket_rows] = far_pair[...]
    left, right = hidden[:, 0, :], hidden[:, 1, :]
    same = jnp.where(side == 0, left, right).astype(jnp.bfloat16)
    next_to = jnp.where(side == 0, right, left).astype(jnp.bfloat16)
    pieces = []
    for mine in (True, False):
        for one in (same, next_to):
            first, last = one[:slots], one[slots:]
            chosen = jnp.where((core == 0) == mine, first, last)
            pieces.append(chosen[:, :16])
    near, far = (jnp.concatenate(two, axis=1) for two in (pieces[:2], pieces[2:]))
    step = 8
    for start in range(0, out.shape[1], step):
        columns = slice(start * HD, (start + step) * HD)
        block = jnp.dot(near, near_rows[:, columns], preferred_element_type=jnp.float32)
        block += jnp.dot(far, rows[:, columns], preferred_element_type=jnp.float32)
        for i in range(step):
            wide[:, start + i, :] = block[:, i * HD : (i + 1) * HD]
    out[...] = wide[...].astype(jnp.bfloat16)


def reduce_kernel(received, out):
    total = received[0].astype(jnp.float32)
    for i in range(1, received.shape[0]):
        total += received[i].astype(jnp.float32)
    total = total.astype(jnp.bfloat16)
    for i in range(out.shape[0]):
        out[i] = total


def steps_kernel(
    length, shares, cosine, sine, first_query, fresh, cache, other, own_keys, out, made,
    own_values, held, kept, semaphore,
):
    core = lax.axis_index("core")
    chip = lax.axis_index(CHIPS)
    positions = own_keys.shape[0]
    copy = pltpu.make_async_copy(cache.at[core, 1], own_values, semaphore)
    copy.start()
    rows = 2 * QH

    @pl.when(chip >= 0)
    def _():
        projected = shares[0].astype(jnp.float32)
        for i in range(1, shares.shape[0]):
            projected += shares[i].astype(jnp.float32)
        turned = projected[: QH + KVH]
        turned = turned * cosine[...] + pltpu.roll(turned, HD // 2, 1) * sine[...]
        second = jnp.concatenate([turned[QH:], projected[QH + KVH :]], axis=0)
        query = joint(first_query[...].astype(jnp.float32), turned[:QH]).astype(jnp.bfloat16)
        limit = length[:, 0:1]
        parts = [
            scored(query, other.at[0], (chip * 2 + 1 - core) * positions, limit),
            scored(query, own_keys, (chip * 2 + core) * positions, limit),
        ]

        wide = query.astype(jnp.float32)
        rows = 2 * QH
        step = (lax.broadcasted_iota(jnp.int32, (rows, 1), 0) // GROUP) % 2
        earlier = fresh[...].astype(jnp.float32)
        later = second.astype(jnp.bfloat16).astype(jnp.float32)
        extras = []
        for token, counted in ((earlier, step >= 0), (later, step == 1)):
            score = jnp.sum(wide * spread(token[:KVH]), axis=1, keepdims=True) * HD ** (-0.5)
            extras.append(jnp.where(counted & (chip == 0), score, MASKED))

        biggest = jnp.maximum(extras[0], extras[1])
        for part in parts:
            biggest = jnp.maximum(biggest, jnp.max(part, axis=1, keepdims=True))
        total = jnp.zeros((rows, 1), jnp.float32)
        summed = jnp.zeros((rows, HD), jnp.float32)
        for score, token in zip(extras, (earlier, later)):
            exponential = jnp.where(score > 0.5 * MASKED, jnp.exp(score - biggest), 0.0)
            total += exponential
            summed += exponential.astype(jnp.bfloat16).astype(jnp.float32) * spread(token[KVH:])
        rounded = []
        for part in parts:
            exponentials = jnp.where(part > 0.5 * MASKED, jnp.exp(part - biggest), 0.0)
            total += jnp.sum(exponentials, axis=1, keepdims=True)
            rounded.append(exponentials.astype(jnp.bfloat16))
        summed += weighted(rounded[0], other.at[1])
        used = total > 0.0
        safe = jnp.where(used, total, 1.0)
        held[0] = summed
        held[1] = jnp.broadcast_to(1.0 / safe, (rows, HD))
        weights = as_row(by_step(jnp.where(used, biggest + jnp.log(safe), MASKED)))
        high = weights.astype(jnp.bfloat16).astype(jnp.float32)
        middle = (weights - high).astype(jnp.bfloat16).astype(jnp.float32)
        low = weights - high - middle
        made[...] = second.astype(jnp.bfloat16)
        tail = jnp.concatenate([high, middle, low, jnp.zeros((5, HD), jnp.float32)], axis=0)
        tail = tail.astype(jnp.bfloat16)
        for i in range(out.shape[0]):
            out[i, rows:] = tail
        kept[...] = rounded[1]

    @pl.when(chip >= 0)
    def _():
        copy.wait()
        attended = (held[0] + weighted(kept[...], own_values)) * held[1]
        attended = by_step(attended).astype(jnp.bfloat16)
        for i in range(out.shape[0]):
            out[i, :rows] = attended


def flat(rows):
    return jnp.concatenate([rows[i : i + 1] for i in range(rows.shape[0])], axis=1)


def combine_kernel(shares, made, out):
    rows = 2 * QH
    weights = []
    for i in range(shares.shape[0]):
        pieces = shares[i, rows:].astype(jnp.float32)
        weights.append(as_column(pieces[0:1] + pieces[1:2] + pieces[2:3], rows))
    biggest = weights[0]
    for weight in weights[1:]:
        biggest = jnp.maximum(biggest, weight)
    total = jnp.zeros((rows, 1), jnp.float32)
    summed = jnp.zeros((rows, HD), jnp.float32)
    for i, weight in enumerate(weights):
        scale = jnp.exp(weight - biggest)
        total += scale
        summed += scale * shares[i, :rows].astype(jnp.float32)
    out[:rows] = (summed / total).astype(jnp.bfloat16)
    out[rows:] = made[...]


def assemble_kernel(mine, theirs, attended, made):
    core = lax.axis_index("core")
    own, other = mine[...].astype(jnp.float32), theirs[...].astype(jnp.float32)
    fresh = []
    for rows in (jnp.where(core == 0, own, other), jnp.where(core == 0, other, own)):
        attended[len(fresh)] = jnp.concatenate(
            [flat(rows[:QH]), flat(rows[QH : 2 * QH])], axis=0
        ).astype(jnp.bfloat16)
        fresh.append(flat(rows[2 * QH :]))
    made[...] = jnp.concatenate(fresh, axis=0).astype(jnp.bfloat16)


def kernel_call(
    kernel, out_shape, name, operands, spaces="", scratch=(), limit=VMEM_BYTES, work=0
):
    kinds = {"v": pltpu.VMEM, "s": pltpu.SMEM, "h": pltpu.HBM}
    spaces = spaces or "v" * len(operands)
    moved = sum(one.size * one.dtype.itemsize for one in (*operands, *out_shape))
    return pl.pallas_call(
        kernel,
        in_specs=[pl.BlockSpec(memory_space=kinds[one]) for one in spaces],
        out_specs=[pl.BlockSpec(memory_space=pltpu.VMEM)] * len(out_shape),
        out_shape=out_shape,
        scratch_shapes=scratch,
        compiler_params=pltpu.CompilerParams(vmem_limit_bytes=limit),
        cost_estimate=pl.CostEstimate(flops=work, bytes_accessed=moved, transcendentals=0),
        name=name,
    )(*operands)


def swap(value):
    return lax.ppermute(value, "core", [(0, 1), (1, 0)])


def local(q_first, kv_first, hidden_next, lengths, owners, sectioned, kv_cache):
    rep_size = lax.axis_size(REP)
    folded = lax.axis_size(FOLD)
    chips = lax.axis_size(CHIPS)
    core = lax.axis_index("core")
    bf16, f32 = jnp.bfloat16, jnp.float32
    shape = jax.ShapeDtypeStruct
    _, _, positions, columns = kv_cache.shape

    (by_slot,) = kernel_call(
        route_kernel,
        (shape((rep_size, 4, HD), f32),),
        "route_hidden",
        (hidden_next, owners),
        limit=ALL_VMEM,
    )
    by_slot, sectioned, kv_cache = lax.optimization_barrier((by_slot, sectioned, kv_cache))
    hidden = lax.all_to_all(by_slot, ("core",) + FOLD, 0, 0, tiled=True)
    pair_rows = lax.ppermute(sectioned[0], "yq", [(0, 1), (1, 0)])
    far_rows = swap(sectioned[0])
    far_pair = swap(pair_rows)
    (near_rows,) = kernel_call(
        pack_kernel,
        (shape((32, HEADS * HD), bf16),),
        "pack_rows",
        (sectioned[0], pair_rows),
    )
    hidden, near_rows, far_rows, far_pair = lax.optimization_barrier(
        (hidden, near_rows, far_rows, far_pair)
    )
    (partial_sum,) = kernel_call(
        project_kernel,
        (shape((folded, HEADS, HD), bf16),),
        "project",
        (hidden, near_rows, far_rows, far_pair),
        scratch=[
            pltpu.VMEM((32, HEADS * HD), bf16),
            pltpu.VMEM((folded, HEADS, HD), f32),
        ],
    )
    partial_sum, kv_cache = lax.optimization_barrier((partial_sum, kv_cache))
    received = lax.all_to_all(partial_sum, FOLD, 0, 0, tiled=True)

    own_keys, staged = pl.pallas_call(
        fetch_kernel,
        in_specs=[pl.BlockSpec(memory_space=pltpu.HBM)],
        out_specs=[pl.BlockSpec(memory_space=pltpu.VMEM), pl.BlockSpec(memory_space=pltpu.HBM)],
        out_shape=(shape((positions, columns), bf16), shape(kv_cache.shape[1:], bf16)),
        scratch_shapes=[
            pltpu.VMEM(kv_cache.shape[1:], bf16),
            pltpu.SemaphoreType.DMA((4,)),
            pltpu.SemaphoreType.DMA((4,)),
            pltpu.SemaphoreType.DMA,
        ],
        compiler_params=pltpu.CompilerParams(vmem_limit_bytes=52 * 1024 * 1024),
        name="fetch_cache",
    )(kv_cache)
    other_cache = swap(staged)
    lengths, own_keys = lax.optimization_barrier((lengths, own_keys))
    halved = np.float32(1000000.0) ** (-(np.arange(HD // 2, dtype=np.float32) * 2.0 / HD))
    frequency = jnp.asarray(np.concatenate([halved, halved])[None], f32)
    length, cosine, sine, query, fresh = kernel_call(
        prepare_kernel,
        (
            shape((1, HD), jnp.int32),
            shape((1, HD), f32),
            shape((1, HD), f32),
            shape((QH, HD), bf16),
            shape((2 * KVH, HD), bf16),
        ),
        "prepare_rows",
        (lengths, q_first, kv_first, frequency),
        spaces="svvv",
    )
    received, length = lax.optimization_barrier((received, length))
    (reduced,) = kernel_call(
        reduce_kernel,
        (shape((chips, HEADS, HD), bf16),),
        "sum_over_replicas",
        (received,),
        work=BETWEEN,
    )
    shares = lax.all_to_all(reduced, CHIPS, 0, 0, tiled=True)
    payload, made = kernel_call(
        steps_kernel,
        (shape((chips, 2 * QH + 8, HD), bf16), shape((2 * KVH, HD), bf16)),
        "both_steps",
        (length, shares, cosine, sine, query, fresh, kv_cache, other_cache, own_keys),
        spaces="vvvvvvhvv",
        scratch=[
            pltpu.VMEM((positions, columns), bf16),
            pltpu.VMEM((2, 2 * QH, HD), f32),
            pltpu.VMEM((2 * QH, positions), bf16),
            pltpu.SemaphoreType.DMA,
        ],
        limit=MOST_VMEM,
    )
    gathered = lax.all_to_all(payload, CHIPS, 0, 0, tiled=True)
    (mine,) = kernel_call(
        combine_kernel,
        (shape((2 * QH + 2 * KVH, HD), bf16),),
        "combine",
        (gathered, made),
    )
    attended, made = kernel_call(
        assemble_kernel,
        (shape((2, 2, QH * HD), bf16), shape((2, 2 * KVH * HD), bf16)),
        "assemble",
        (mine, swap(mine)),
    )
    return attended, made


def solution(mesh):
    fine = Mesh(mesh.devices.reshape(2, 2, 8, 2, 4, 2), ("yp", "yq", "z", "yh", "x", "core"))
    placed = (
        P(REP, None),
        P(REP, None),
        P(REP, CTX),
        P(REP),
        P(CTX, None),
        P(REP, CTX, None),
        P(REP, None, CTX, None),
    )
    return jax.shard_map(
        local,
        mesh=fine,
        in_specs=placed,
        out_specs=(P(REP, None, None), P(REP, None)),
        check_vma=False,
    )
```

```python
import jax
import jax.numpy as jnp
import numpy as np
from jax import lax
from jax.experimental import pallas as pl
from jax.experimental.pallas import tpu as pltpu
from jax.sharding import Mesh, PartitionSpec as P

HD = 128
QH = 32
KVH = 4
GROUP = QH // KVH
HEADS = QH + 2 * KVH
REP = ("yp", "yq", "z")
FOLD = ("yq", "z")
CHIPS = ("yh", "x")
CTX = ("yh", "x", "core")
MASKED = -3e38
VMEM_BYTES = 16 * 1024 * 1024
BETWEEN = 1 << 36
MOST_VMEM = 48 * 1024 * 1024
ALL_VMEM = 60 * 1024 * 1024


def spread(rows):
    return jnp.concatenate(
        [jnp.broadcast_to(rows[g : g + 1], (2 * GROUP, HD)) for g in range(KVH)], axis=0
    )


def joint(first, second):
    pieces = []
    for g in range(KVH):
        pieces += [first[g * GROUP : (g + 1) * GROUP], second[g * GROUP : (g + 1) * GROUP]]
    return jnp.concatenate(pieces, axis=0)


def by_step(rows):
    return jnp.concatenate(
        [
            rows[(2 * g + step) * GROUP : (2 * g + step + 1) * GROUP]
            for step in range(2)
            for g in range(KVH)
        ],
        axis=0,
    )


def scored(query, keys, start, length):
    scores = jnp.concatenate(
        [
            lax.dot_general(
                query[2 * g * GROUP : 2 * (g + 1) * GROUP],
                keys[:, g * HD : (g + 1) * HD],
                (((1,), (1,)), ((), ())),
                preferred_element_type=jnp.float32,
            )
            for g in range(KVH)
        ],
        axis=0,
    ) * HD ** (-0.5)
    position = start + lax.broadcasted_iota(jnp.int32, (1, keys.shape[0]), 1)
    return jnp.where(position < length, scores, MASKED)


def weighted(rounded, values):
    return jnp.concatenate(
        [
            jnp.dot(
                rounded[2 * g * GROUP : 2 * (g + 1) * GROUP],
                values[:, g * HD : (g + 1) * HD],
                preferred_element_type=jnp.float32,
            )
            for g in range(KVH)
        ],
        axis=0,
    )


def as_row(column):
    rows = column.shape[0]
    diagonal = lax.broadcasted_iota(jnp.int32, (rows, HD), 0) == lax.broadcasted_iota(
        jnp.int32, (rows, HD), 1
    )
    return jnp.sum(jnp.where(diagonal, column, 0.0), axis=0, keepdims=True)


def pad_lanes(row):
    return jnp.concatenate([row, jnp.zeros((1, HD - row.shape[1]), row.dtype)], axis=1)


def as_column(row, rows):
    diagonal = lax.broadcasted_iota(jnp.int32, (rows, HD), 0) == lax.broadcasted_iota(
        jnp.int32, (rows, HD), 1
    )
    return jnp.sum(jnp.where(diagonal, row, 0.0), axis=1, keepdims=True)


def fetch_kernel(cache, own_keys, other, scratch, arrived, left, semaphore):
    core = lax.axis_index("core")
    parts = arrived.shape[0] // 2
    rows = cache.shape[2] // parts
    pieces = [(kind, pl.ds(part * rows, rows)) for kind in range(2) for part in range(parts)]
    inward = [
        pltpu.make_async_copy(cache.at[1 - core, kind, block], scratch.at[kind, block], arrived.at[i])
        for i, (kind, block) in enumerate(pieces)
    ]
    outward = [
        pltpu.make_async_copy(scratch.at[kind, block], other.at[kind, block], left.at[i])
        for i, (kind, block) in enumerate(pieces)
    ]
    own = pltpu.make_async_copy(cache.at[core, 0], own_keys, semaphore)
    for copy in (*inward, own):
        copy.start()
    for first, second in zip(inward, outward):
        first.wait()
        second.start()
    own.wait()
    for copy in outward:
        copy.wait()


def prepare_kernel(lengths, queries, fresh, frequency, length, cosine, sine, query, new_rows):
    core = lax.axis_index("core")
    length[...] = jnp.zeros_like(length) + lengths[core]
    angles = (lengths[core] + 1).astype(jnp.float32) * frequency[...]
    lane = lax.broadcasted_iota(jnp.int32, (1, HD), 1)
    cosine[...] = jnp.cos(angles)
    sine[...] = jnp.where(lane < HD // 2, -1.0, 1.0) * jnp.sin(angles)
    wide = queries[...].astype(jnp.float32)
    wide = jnp.where(core == 0, wide[0:1], wide[1:2])
    query[...] = jnp.concatenate(
        [wide[:, i * HD : (i + 1) * HD] for i in range(QH)], axis=0
    ).astype(jnp.bfloat16)
    wide = fresh[...].astype(jnp.float32)
    wide = jnp.where(core == 0, wide[0:1], wide[1:2])
    new_rows[...] = jnp.concatenate(
        [wide[:, i * HD : (i + 1) * HD] for i in range(2 * KVH)], axis=0
    ).astype(jnp.bfloat16)


def route_kernel(hidden, owners, out):
    slots = owners.shape[1]
    columns = hidden.shape[1]
    bucket_rows = columns // slots
    column = lax.broadcasted_iota(jnp.int32, (slots, columns), 1)
    first = lax.broadcasted_iota(jnp.int32, (slots, columns), 0) * bucket_rows
    inside = (column >= first) & (column < first + bucket_rows)
    owner = jnp.sum(
        jnp.where(inside, as_column(pad_lanes(owners[...].astype(jnp.float32)), slots), 0.0),
        axis=0,
        keepdims=True,
    )
    chosen = owner == lax.broadcasted_iota(jnp.int32, (slots, columns), 0).astype(jnp.float32)
    row = lax.broadcasted_iota(jnp.int32, (columns, HD), 0)
    lane = lax.broadcasted_iota(jnp.int32, (columns, HD), 1)
    bucket = jnp.floor((row.astype(jnp.float32) + 0.5) * (1.0 / bucket_rows)).astype(jnp.int32)
    fold = row == lane + bucket * bucket_rows
    fold = jnp.where(fold, 1.0, 0.0).astype(jnp.bfloat16)
    for core in range(2):
        kept = jnp.where(chosen, hidden[core : core + 1].astype(jnp.float32), 0.0)
        folded = jnp.dot(kept.astype(jnp.bfloat16), fold, preferred_element_type=jnp.float32)
        column_size = slots // 4
        for outer in range(2):
            first = (2 * core + outer) * column_size
            for pair in range(2):
                block = (2 * pair + outer) * column_size
                out[first : first + column_size, pair, :] = folded[block : block + column_size]


def pack_kernel(own_rows, pair_rows, near_rows):
    bucket_rows = own_rows.shape[0]
    near_rows[...] = jnp.zeros_like(near_rows)
    near_rows[0:bucket_rows] = own_rows[...]
    near_rows[16 : 16 + bucket_rows] = pair_rows[...]


def project_kernel(hidden, near_rows, far_rows, far_pair, out, rows, wide):
    core = lax.axis_index("core")
    side = lax.axis_index("yp")
    bucket_rows = far_rows.shape[0]
    slots = out.shape[0]
    rows[...] = jnp.zeros_like(rows)
    rows[0:bucket_rows] = far_rows[...]
    rows[16 : 16 + bucket_rows] = far_pair[...]
    left, right = hidden[:, 0, :], hidden[:, 1, :]
    same = jnp.where(side == 0, left, right).astype(jnp.bfloat16)
    next_to = jnp.where(side == 0, right, left).astype(jnp.bfloat16)
    pieces = []
    for mine in (True, False):
        for one in (same, next_to):
            first, last = one[:slots], one[slots:]
            chosen = jnp.where((core == 0) == mine, first, last)
            pieces.append(chosen[:, :16])
    near, far = (jnp.concatenate(two, axis=1) for two in (pieces[:2], pieces[2:]))
    step = 8
    for start in range(0, out.shape[1], step):
        columns = slice(start * HD, (start + step) * HD)
        block = jnp.dot(near, near_rows[:, columns], preferred_element_type=jnp.float32)
        block += jnp.dot(far, rows[:, columns], preferred_element_type=jnp.float32)
        for i in range(step):
            wide[:, start + i, :] = block[:, i * HD : (i + 1) * HD]
    out[...] = wide[...].astype(jnp.bfloat16)


def reduce_kernel(received, out):
    total = received[0].astype(jnp.float32)
    for i in range(1, received.shape[0]):
        total += received[i].astype(jnp.float32)
    total = total.astype(jnp.bfloat16)
    for i in range(out.shape[0]):
        out[i] = total


def steps_kernel(
    length, shares, cosine, sine, first_query, fresh, cache, other, own_keys, out, made,
    own_values, held, kept, semaphore,
):
    core = lax.axis_index("core")
    chip = lax.axis_index(CHIPS)
    positions = own_keys.shape[0]
    copy = pltpu.make_async_copy(cache.at[core, 1], own_values, semaphore)
    copy.start()
    rows = 2 * QH

    @pl.when(chip >= 0)
    def _():
        projected = shares[0].astype(jnp.float32)
        for i in range(1, shares.shape[0]):
            projected += shares[i].astype(jnp.float32)
        turned = projected[: QH + KVH]
        turned = turned * cosine[...] + pltpu.roll(turned, HD // 2, 1) * sine[...]
        second = jnp.concatenate([turned[QH:], projected[QH + KVH :]], axis=0)
        query = joint(first_query[...].astype(jnp.float32), turned[:QH]).astype(jnp.bfloat16)
        limit = length[:, 0:1]
        parts = [
            scored(query, other.at[0], (chip * 2 + 1 - core) * positions, limit),
            scored(query, own_keys, (chip * 2 + core) * positions, limit),
        ]

        wide = query.astype(jnp.float32)
        rows = 2 * QH
        step = (lax.broadcasted_iota(jnp.int32, (rows, 1), 0) // GROUP) % 2
        earlier = fresh[...].astype(jnp.float32)
        later = second.astype(jnp.bfloat16).astype(jnp.float32)
        extras = []
        for token, counted in ((earlier, step >= 0), (later, step == 1)):
            score = jnp.sum(wide * spread(token[:KVH]), axis=1, keepdims=True) * HD ** (-0.5)
            extras.append(jnp.where(counted & (chip == 0), score, MASKED))

        biggest = jnp.maximum(extras[0], extras[1])
        for part in parts:
            biggest = jnp.maximum(biggest, jnp.max(part, axis=1, keepdims=True))
        total = jnp.zeros((rows, 1), jnp.float32)
        summed = jnp.zeros((rows, HD), jnp.float32)
        for score, token in zip(extras, (earlier, later)):
            exponential = jnp.where(score > 0.5 * MASKED, jnp.exp(score - biggest), 0.0)
            total += exponential
            summed += exponential.astype(jnp.bfloat16).astype(jnp.float32) * spread(token[KVH:])
        rounded = []
        for part in parts:
            exponentials = jnp.where(part > 0.5 * MASKED, jnp.exp(part - biggest), 0.0)
            total += jnp.sum(exponentials, axis=1, keepdims=True)
            rounded.append(exponentials.astype(jnp.bfloat16))
        summed += weighted(rounded[0], other.at[1])
        used = total > 0.0
        safe = jnp.where(used, total, 1.0)
        held[0] = summed
        held[1] = jnp.broadcast_to(1.0 / safe, (rows, HD))
        weights = as_row(by_step(jnp.where(used, biggest + jnp.log(safe), MASKED)))
        high = weights.astype(jnp.bfloat16).astype(jnp.float32)
        middle = (weights - high).astype(jnp.bfloat16).astype(jnp.float32)
        low = weights - high - middle
        made[...] = second.astype(jnp.bfloat16)
        tail = jnp.concatenate([high, middle, low, jnp.zeros((5, HD), jnp.float32)], axis=0)
        tail = tail.astype(jnp.bfloat16)
        for i in range(out.shape[0]):
            out[i, rows:] = tail
        kept[...] = rounded[1]

    @pl.when(chip >= 0)
    def _():
        copy.wait()
        attended = (held[0] + weighted(kept[...], own_values)) * held[1]
        attended = by_step(attended).astype(jnp.bfloat16)
        for i in range(out.shape[0]):
            out[i, :rows] = attended


def flat(rows):
    return jnp.concatenate([rows[i : i + 1] for i in range(rows.shape[0])], axis=1)


def combine_kernel(shares, made, out):
    rows = 2 * QH
    weights = []
    for i in range(shares.shape[0]):
        pieces = shares[i, rows:].astype(jnp.float32)
        weights.append(as_column(pieces[0:1] + pieces[1:2] + pieces[2:3], rows))
    biggest = weights[0]
    for weight in weights[1:]:
        biggest = jnp.maximum(biggest, weight)
    total = jnp.zeros((rows, 1), jnp.float32)
    summed = jnp.zeros((rows, HD), jnp.float32)
    for i, weight in enumerate(weights):
        scale = jnp.exp(weight - biggest)
        total += scale
        summed += scale * shares[i, :rows].astype(jnp.float32)
    out[:rows] = (summed / total).astype(jnp.bfloat16)
    out[rows:] = made[...]


def assemble_kernel(mine, theirs, attended, made):
    core = lax.axis_index("core")
    own, other = mine[...].astype(jnp.float32), theirs[...].astype(jnp.float32)
    fresh = []
    for rows in (jnp.where(core == 0, own, other), jnp.where(core == 0, other, own)):
        attended[len(fresh)] = jnp.concatenate(
            [flat(rows[:QH]), flat(rows[QH : 2 * QH])], axis=0
        ).astype(jnp.bfloat16)
        fresh.append(flat(rows[2 * QH :]))
    made[...] = jnp.concatenate(fresh, axis=0).astype(jnp.bfloat16)


def kernel_call(
    kernel, out_shape, name, operands, spaces="", scratch=(), limit=VMEM_BYTES, work=0
):
    kinds = {"v": pltpu.VMEM, "s": pltpu.SMEM, "h": pltpu.HBM}
    spaces = spaces or "v" * len(operands)
    moved = sum(one.size * one.dtype.itemsize for one in (*operands, *out_shape))
    return pl.pallas_call(
        kernel,
        in_specs=[pl.BlockSpec(memory_space=kinds[one]) for one in spaces],
        out_specs=[pl.BlockSpec(memory_space=pltpu.VMEM)] * len(out_shape),
        out_shape=out_shape,
        scratch_shapes=scratch,
        compiler_params=pltpu.CompilerParams(vmem_limit_bytes=limit),
        cost_estimate=pl.CostEstimate(flops=work, bytes_accessed=moved, transcendentals=0),
        name=name,
    )(*operands)


def swap(value):
    return lax.ppermute(value, "core", [(0, 1), (1, 0)])


def local(q_first, kv_first, hidden_next, lengths, owners, sectioned, kv_cache):
    rep_size = lax.axis_size(REP)
    folded = lax.axis_size(FOLD)
    chips = lax.axis_size(CHIPS)
    core = lax.axis_index("core")
    bf16, f32 = jnp.bfloat16, jnp.float32
    shape = jax.ShapeDtypeStruct
    _, _, positions, columns = kv_cache.shape

    (by_slot,) = kernel_call(
        route_kernel,
        (shape((rep_size, 4, HD), f32),),
        "route_hidden",
        (hidden_next, owners),
        limit=ALL_VMEM,
    )
    by_slot, sectioned, kv_cache = lax.optimization_barrier((by_slot, sectioned, kv_cache))
    hidden = lax.all_to_all(by_slot, ("core",) + FOLD, 0, 0, tiled=True)
    pair_rows = lax.ppermute(sectioned[0], "yp", [(0, 1), (1, 0)])
    far_rows = swap(sectioned[0])
    far_pair = swap(pair_rows)
    (near_rows,) = kernel_call(
        pack_kernel,
        (shape((32, HEADS * HD), bf16),),
        "pack_rows",
        (sectioned[0], pair_rows),
    )
    hidden, near_rows, far_rows, far_pair = lax.optimization_barrier(
        (hidden, near_rows, far_rows, far_pair)
    )
    (partial_sum,) = kernel_call(
        project_kernel,
        (shape((folded, HEADS, HD), bf16),),
        "project",
        (hidden, near_rows, far_rows, far_pair),
        scratch=[
            pltpu.VMEM((32, HEADS * HD), bf16),
            pltpu.VMEM((folded, HEADS, HD), f32),
        ],
    )
    partial_sum, kv_cache = lax.optimization_barrier((partial_sum, kv_cache))
    received = lax.all_to_all(partial_sum, FOLD, 0, 0, tiled=True)

    own_keys, staged = pl.pallas_call(
        fetch_kernel,
        in_specs=[pl.BlockSpec(memory_space=pltpu.HBM)],
        out_specs=[pl.BlockSpec(memory_space=pltpu.VMEM), pl.BlockSpec(memory_space=pltpu.HBM)],
        out_shape=(shape((positions, columns), bf16), shape(kv_cache.shape[1:], bf16)),
        scratch_shapes=[
            pltpu.VMEM(kv_cache.shape[1:], bf16),
            pltpu.SemaphoreType.DMA((4,)),
            pltpu.SemaphoreType.DMA((4,)),
            pltpu.SemaphoreType.DMA,
        ],
        compiler_params=pltpu.CompilerParams(vmem_limit_bytes=52 * 1024 * 1024),
        name="fetch_cache",
    )(kv_cache)
    other_cache = swap(staged)
    lengths, own_keys = lax.optimization_barrier((lengths, own_keys))
    halved = np.float32(1000000.0) ** (-(np.arange(HD // 2, dtype=np.float32) * 2.0 / HD))
    frequency = jnp.asarray(np.concatenate([halved, halved])[None], f32)
    length, cosine, sine, query, fresh = kernel_call(
        prepare_kernel,
        (
            shape((1, HD), jnp.int32),
            shape((1, HD), f32),
            shape((1, HD), f32),
            shape((QH, HD), bf16),
            shape((2 * KVH, HD), bf16),
        ),
        "prepare_rows",
        (lengths, q_first, kv_first, frequency),
        spaces="svvv",
    )
    received, length = lax.optimization_barrier((received, length))
    (reduced,) = kernel_call(
        reduce_kernel,
        (shape((chips, HEADS, HD), bf16),),
        "sum_over_replicas",
        (received,),
        work=BETWEEN,
    )
    shares = lax.all_to_all(reduced, CHIPS, 0, 0, tiled=True)
    payload, made = kernel_call(
        steps_kernel,
        (shape((chips, 2 * QH + 8, HD), bf16), shape((2 * KVH, HD), bf16)),
        "both_steps",
        (length, shares, cosine, sine, query, fresh, kv_cache, other_cache, own_keys),
        spaces="vvvvvvhvv",
        scratch=[
            pltpu.VMEM((positions, columns), bf16),
            pltpu.VMEM((2, 2 * QH, HD), f32),
            pltpu.VMEM((2 * QH, positions), bf16),
            pltpu.SemaphoreType.DMA,
        ],
        limit=MOST_VMEM,
    )
    gathered = lax.all_to_all(payload, CHIPS, 0, 0, tiled=True)
    (mine,) = kernel_call(
        combine_kernel,
        (shape((2 * QH + 2 * KVH, HD), bf16),),
        "combine",
        (gathered, made),
    )
    attended, made = kernel_call(
        assemble_kernel,
        (shape((2, 2, QH * HD), bf16), shape((2, 2 * KVH * HD), bf16)),
        "assemble",
        (mine, swap(mine)),
    )
    return attended, made


def solution(mesh):
    fine = Mesh(mesh.devices.reshape(2, 2, 8, 2, 4, 2), ("yp", "yq", "z", "yh", "x", "core"))
    placed = (
        P(REP, None),
        P(REP, None),
        P(REP, CTX),
        P(REP),
        P(CTX, None),
        P(REP, CTX, None),
        P(REP, None, CTX, None),
    )
    return jax.shard_map(
        local,
        mesh=fine,
        in_specs=placed,
        out_specs=(P(REP, None, None), P(REP, None)),
        check_vma=False,
    )
```
